128 devices in a mesh: dp: 8 (over y, z_lo), ctx: 16 (over x, z_hi, core).
Axes of the slice: x: 4, y: 4, z: 4 (z_hi: 2, z_lo: 2; z = z_hi * 2 + z_lo), core: 2. Of those that a mesh axis runs over, the one named last changes fastest.
Arguments:
- uvqk: bfloat16 [8, 2048, 4096], P('dp', 'ctx'), may hold values from -6 to 6
- residual: bfloat16 [8, 2048, 1024], P('dp', 'ctx'), may hold values from -6 to 6
- lengths: int32 [8, 8], P('dp'), may hold values from 1 to 1024, 2048 in all within a row
- time_buckets: int32 [8, 2048], P('dp', 'ctx'), may hold values from 0 to 15
- pos_table: float32 [8, 16], replicated, may hold values from -4 to 4
- time_table: float32 [8, 16], replicated, may hold values from -4 to 4
- output_norm_gain: float32 [1024], replicated, may hold values from 0.5 to 1.5
- w_out: bfloat16 [1024, 1024], replicated, may hold values from -0.1875 to 0.1875
- cotangent: bfloat16 [8, 2048, 1024], P('dp', 'ctx'), may hold values from -6 to 6
Outputs:
- layer_out: bfloat16 [8, 2048, 1024], P('dp', 'ctx')
- d_uvqk: bfloat16 [8, 2048, 4096], P('dp', 'ctx')
- d_w_out: float32 [1024, 1024], P(('dp', 'ctx'))
- d_norm_gain: float32 [1024], replicated
- d_pos_table: float32 [8, 16], replicated
- d_time_table: float32 [8, 16], replicated
The draws below stay inside these ranges and needn't reach their ends.
Inputs may be any that keep to these rules, and one draw needn't show every extreme that they name: `lengths`: each row sums to 2048, and its largest entry is exactly 1024.
All inputs are finite; a program needn't handle non-finite values.
Results may differ from the reference program's by a relative error of at most 0.0066.
Values may be sent and summed in bfloat16 or wider, within the bound.
A program may use at most 128 MiB of HBM per device.

```python
import math
import jax
import jax.numpy as jnp
import numpy as np
from jax import lax

D = 1024
HEADS = 8
TOK_DEV = 128
USERS = 8
PB = 16
TB = 16
SEQ = 2048
MAXLEN = 1024
BATCH = 8
N_CTX = 16


def place_ends(array, own_key, least, high):
    longest = array.shape.index(max(array.shape))
    spots = []
    for shift in (0, 1):
        where = [jax.random.randint(jax.random.fold_in(own_key, axis), (), 0, length) for axis, length in enumerate(array.shape)]
        where[longest] = (where[longest] + shift) % array.shape[longest]
        spots.append(tuple(where))
    return array.at[spots[0]].set(least).at[spots[1]].set(high)


def block_levels(own_key, extent, shards, least, largest):
    factor_of = 1.0
    for axis_at, blocks in shards:
        heights = jax.random.uniform(jax.random.fold_in(jax.random.fold_in(own_key, 6), axis_at), (blocks,), jnp.float32, least / len(shards), largest / len(shards))
        factor_of = factor_of * jnp.repeat(jnp.exp(heights), extent[axis_at] // blocks).reshape((-1,) + (1,) * (len(extent) - 1 - axis_at))
    return factor_of


def profile(amount, total, bound, slope):
    weights = [(1 << 20) // math.isqrt(grade ** slope) + 1 for grade in range(2, amount + 1)]
    surplus, counts = total - bound - (amount - 1), [1] * (amount - 1)
    while surplus > 0:
        movable = [i for i in range(amount - 1) if counts[i] < bound]
        mass, remaining = sum([weights[i] for i in movable]), surplus
        for i in movable:
            extra = min(bound - counts[i], max(1, remaining * weights[i] // mass), surplus)
            counts[i] = counts[i] + extra
            surplus = surplus - extra
    return np.array([bound] + counts)


def ragged_sizes(stream_key, amount, total, reach, slope):
    if amount == 2:
        one = jax.random.randint(stream_key, (), max(1, total - reach), min(reach, total - 1) + 1)
        return jnp.stack([one, total - one])
    tallies = jnp.asarray(profile(amount, total, reach, slope), jnp.int32)
    pairs = (amount - 1) // 2
    donor, sink = tallies[1:1 + 2 * pairs:2], tallies[2:2 + 2 * pairs:2]
    slack = jnp.minimum(donor - 1, reach - sink)
    shifted = jax.random.randint(jax.random.fold_in(stream_key, 1), (pairs,), 0, 1 << 20) % (slack + 1)
    tallies = tallies.at[1:1 + 2 * pairs:2].set(donor - shifted).at[2:2 + 2 * pairs:2].set(sink + shifted)
    return tallies[jax.random.permutation(jax.random.fold_in(stream_key, 2), amount)]


def gaussian(own_key, extent, spread, most, cuts=(), kind=jnp.bfloat16):
    loudness = block_levels(own_key, extent, cuts, -0.22, 0.18) if cuts else 1.0
    array = jax.random.normal(own_key, extent, jnp.float32) * spread * loudness
    return jnp.minimum(jnp.maximum(array, -most), most).astype(kind)


def setup_inputs(seed: int = 0) -> dict:
    key_list = jax.random.split(jax.random.key(seed), 10)
    return {
        "uvqk": gaussian(key_list[0], (BATCH, SEQ, 4 * D), 1.0, 6.0, ((0, 8), (1, 16))),
        "residual": gaussian(key_list[1], (BATCH, SEQ, D), 1.0, 6.0, ((0, 8), (1, 16))),
        "lengths": jax.vmap(lambda own: ragged_sizes(own, USERS, SEQ, MAXLEN, 2))(jax.random.split(key_list[2], BATCH)).reshape((BATCH, USERS)).astype(jnp.int32),
        "time_buckets": place_ends(jax.random.randint(key_list[3], (BATCH, SEQ), 0, TB), jax.random.fold_in(key_list[3], 1), 0, TB - 1).astype(jnp.int32),
        "pos_table": gaussian(key_list[4], (HEADS, PB), 1.0, 4.0, (), jnp.float32),
        "time_table": gaussian(key_list[5], (HEADS, TB), 1.0, 4.0, (), jnp.float32),
        "output_norm_gain": jnp.clip(1.0 + 0.1 * jax.random.normal(key_list[6], (D,), jnp.float32), 0.5, 1.5),
        "w_out": gaussian(key_list[7], (D, D), D ** -0.5, 0.1875),
        "cotangent": gaussian(key_list[8], (BATCH, SEQ, D), 1.0, 6.0, ((0, 8), (1, 16))),
    }


EPS = 1e-05

def silu_grad(value):
    sig = jax.nn.sigmoid(value)
    return sig * (1.0 + value * (1.0 - sig))

def pair_masks(query_pos, key_pos, query_user, key_user, query_time, key_time, buckets, maxlen):
    gap = query_pos[:, None] - key_pos[None, :]
    allowed = jnp.logical_and(query_user[:, None] == key_user[None, :], gap >= 0)
    pos_bucket = jnp.minimum(jnp.maximum(gap, 0) * buckets // maxlen, buckets - 1)
    time_gap = jnp.abs(query_time[:, None] - key_time[None, :])
    return (allowed, pos_bucket, time_gap)

def bias_of(pos_table, time_table, pos_bucket, time_gap):
    total = jnp.zeros((pos_table.shape[0],) + pos_bucket.shape, jnp.float32)
    for bucket in range(pos_table.shape[1]):
        total = total + jnp.where(pos_bucket[None] == bucket, pos_table[:, bucket][:, None, None], 0.0)
    for bucket in range(time_table.shape[1]):
        total = total + jnp.where(time_gap[None] == bucket, time_table[:, bucket][:, None, None], 0.0)
    return total

def table_grad(d_scores, pos_bucket, time_gap, pos_count, time_count):
    columns = [lax.optimization_barrier(jnp.sum(jnp.where(pos_bucket[None] == bucket, d_scores, 0.0), axis=(1, 2))) for bucket in range(pos_count)]
    columns = columns + [lax.optimization_barrier(jnp.sum(jnp.where(time_gap[None] == bucket, d_scores, 0.0), axis=(1, 2))) for bucket in range(time_count)]
    return jnp.stack(columns, axis=1)

def reference(uvqk, residual, lengths, time_buckets, pos_table, time_table, output_norm_gain, w_out, cotangent):
    width = D
    hsize = width // HEADS
    scale = hsize ** (-0.5)

    def rows_of(values, start):
        return lax.dynamic_slice_in_dim(values, start, TOK_DEV, 0)

    def one_pack(carry, inputs):
        weight_sum, gain_sum, table_sum = carry
        pre, resid, lens, times, cot = inputs
        pre_f = pre.astype(jnp.float32)
        act = jax.nn.silu(pre_f).astype(jnp.bfloat16)
        u_act = act[:, :width]
        v_heads = act[:, width:2 * width].astype(jnp.float32).reshape(SEQ, HEADS, hsize)
        q_heads = act[:, 2 * width:3 * width].astype(jnp.float32).reshape(SEQ, HEADS, hsize)
        k_heads = act[:, 3 * width:].astype(jnp.float32).reshape(SEQ, HEADS, hsize)
        ends = jnp.cumsum(lens).astype(jnp.int32)
        positions = jnp.arange(SEQ, dtype=jnp.int32)
        users = lax.optimization_barrier(jnp.sum((positions[:, None] >= ends[None, :]).astype(jnp.int32), axis=1))
        starts = jnp.arange(N_CTX, dtype=jnp.int32) * TOK_DEV

        def block_scores(start):
            allowed, pos_bucket, time_gap = pair_masks(rows_of(positions, start), positions, rows_of(users, start), users, rows_of(times, start), times, PB, MAXLEN)
            bias = bias_of(pos_table, time_table, pos_bucket, time_gap)
            scores = jnp.einsum('qhe,khe->hqk', rows_of(q_heads, start), k_heads) * scale + bias
            return (scores, allowed, pos_bucket, time_gap)

        def forward_block(start):
            scores, allowed, _, _ = block_scores(start)
            weights = jnp.where(allowed[None], jax.nn.silu(scores), 0.0).astype(jnp.bfloat16)
            weights = lax.optimization_barrier(weights).astype(jnp.float32)
            return jnp.einsum('hqk,khe->qhe', weights, v_heads).reshape(TOK_DEV, width)
        attended = lax.map(forward_block, starts).reshape(SEQ, width)
        row_average = lax.optimization_barrier(jnp.mean(attended, axis=1, keepdims=True))
        mean_removed = attended - row_average
        var = lax.optimization_barrier(jnp.mean(mean_removed * mean_removed, axis=1, keepdims=True))
        inverse_deviation = lax.rsqrt(var + EPS)
        standardized_input = mean_removed * inverse_deviation
        normalized_rows = standardized_input * output_norm_gain[None, :]
        u_float = u_act.astype(jnp.float32)
        hidden = (normalized_rows * u_float).astype(jnp.bfloat16)
        output = (resid.astype(jnp.float32) + jnp.dot(hidden, w_out, preferred_element_type=jnp.float32)).astype(jnp.bfloat16)
        weight_term = jnp.dot(hidden.T, cot, preferred_element_type=jnp.float32)
        d_hidden = jnp.dot(cot, w_out.T, preferred_element_type=jnp.float32)
        d_u = d_hidden * normalized_rows
        normalized_gradient = d_hidden * u_float
        gain_product = lax.optimization_barrier(jnp.sum(normalized_gradient * standardized_input, axis=0))
        gain_scaled = normalized_gradient * output_norm_gain[None, :]
        attended_gradient = (inverse_deviation * (gain_scaled - lax.optimization_barrier(jnp.mean(gain_scaled, axis=1, keepdims=True)) - standardized_input * lax.optimization_barrier(jnp.mean(gain_scaled * standardized_input, axis=1, keepdims=True)))).astype(jnp.bfloat16)
        d_heads = attended_gradient.astype(jnp.float32).reshape(SEQ, HEADS, hsize)

        def backward_block(inner, start):
            d_key, d_value, d_table = inner
            scores, allowed, pos_bucket, time_gap = block_scores(start)
            weights = jnp.where(allowed[None], jax.nn.silu(scores), 0.0).astype(jnp.bfloat16)
            weights = lax.optimization_barrier(weights).astype(jnp.float32)
            d_rows = rows_of(d_heads, start)
            d_weights = jnp.einsum('qhe,khe->hqk', d_rows, v_heads)
            d_scores = jnp.where(allowed[None], d_weights * silu_grad(scores), 0.0)
            d_table = d_table + table_grad(d_scores, pos_bucket, time_gap, PB, TB)
            rounded = lax.optimization_barrier(d_scores.astype(jnp.bfloat16)).astype(jnp.float32)
            d_query = jnp.einsum('hqk,khe->qhe', rounded, k_heads) * scale
            d_key = d_key + jnp.einsum('hqk,qhe->khe', rounded, rows_of(q_heads, start)) * scale
            d_value = d_value + jnp.einsum('hqk,qhe->khe', weights, d_rows)
            return ((d_key, d_value, d_table), d_query.reshape(TOK_DEV, width))
        start_inner = (jnp.zeros((SEQ, HEADS, hsize), jnp.float32), jnp.zeros((SEQ, HEADS, hsize), jnp.float32), jnp.zeros((HEADS, PB + TB), jnp.float32))
        (d_key, d_value, table_term), d_query = lax.scan(backward_block, start_inner, starts)
        d_query = d_query.reshape(SEQ, width)
        grads = jnp.concatenate([d_u, d_value.reshape(SEQ, width), d_query, d_key.reshape(SEQ, width)], axis=1)
        d_pre = (grads * silu_grad(pre_f)).astype(jnp.bfloat16)
        return ((weight_sum + weight_term, gain_sum + gain_product, table_sum + table_term), (output, d_pre))
    init = (jnp.zeros((D, D), jnp.float32), jnp.zeros((D,), jnp.float32), jnp.zeros((HEADS, PB + TB), jnp.float32))
    (d_w_out, d_norm_gain, d_table), (layer_out, d_uvqk) = lax.scan(one_pack, init, (uvqk, residual, lengths, time_buckets, cotangent))
    return (layer_out, d_uvqk, d_w_out, d_norm_gain, d_table[:, :PB], d_table[:, PB:])
```

```python
import jax
import jax.numpy as jnp
from jax import lax
from jax.experimental import pallas as pl
from jax.experimental.pallas import tpu as pltpu
from jax.sharding import PartitionSpec as P

MESH = pl.DeviceIdType.MESH
F32 = jnp.float32
BF16 = jnp.bfloat16

HEADS = 8
EPS = 1e-05
ROWS = 128
CHIPS = 8
SPAN = 9
WIN = SPAN * ROWS
PAD = SPAN - 1
WIDTH = HEADS * ROWS
BUCKETS = 16
FAR = 131072.0
SCALE = ROWS ** (-0.5)

KEY, VAL, TIM, QUE, DNO, END = 0, 128, 256, 272, 400, 528
CHUNKS = [(0, 256), (256, 256), (512, 256), (768, 256), (1024, 128)]

NT = (((1,), (1,)), ((), ()))
TN = (((0,), (0,)), ((), ()))
NN = (((1,), (0,)), ((), ()))


def dot(a, b, dims=NN):
    return lax.dot_general(a, b, dims, preferred_element_type=F32)


def exact_dot(a, b, dims=NN):
    return lax.dot_general(
        a, b, dims, preferred_element_type=F32, precision=lax.Precision.HIGHEST
    )


def silu_half(x):
    return x * (1.0 + jnp.tanh(x))


def silu_grad_half(x):
    t = jnp.tanh(x)
    a = 1.0 + t
    return 0.5 * (a + x * a * (1.0 - t))


def columns(h):
    return pl.ds(pl.multiple_of(h * ROWS, ROWS), ROWS)


def kernel(
    uvqk, resid, lens, times, ptab, ttab, gain, wout, cot,
    out, dpre, dwo, dgain, dpos, dtime,
    sb, rb, cot2, dh, kext, vall, aext, wa, pbias, wsave, fsave,
    att_t, pn_t, gcol, att_s, att_r, stats, comb, dout, hid, hid_s, hid2,
    ds_s, ds_r, e_s, e_r, diag, dkv, pacc, tmat, gacc, mq_s, mq_r, xs, xr, mk_s, mk_r,
    tab, tab1, tab2,
    loc_sem, m1s, m1r, m2s, m2r, fws, fwr, sib_s, sib_r, ats, atr, sts, str_,
    d1s, d1r, d2s, d2r, qs, qr, ks, kr, t1s, t1r, t2s, t2r,
):
    dp = lax.axis_index("dp")
    me = lax.axis_index("ctx")
    c = me // 2
    r = me % 2
    y = dp // 2
    zl = dp % 2
    sib = 2 * c + (1 - r)

    def remote(src, dst, ssem, rsem, to):
        return pltpu.make_async_remote_copy(
            src_ref=src, dst_ref=dst, send_sem=ssem, recv_sem=rsem, device_id=to,
            device_id_type=MESH,
        )

    barrier = pltpu.get_barrier_semaphore()

    def greet(j, _):
        pl.semaphore_signal(
            barrier, inc=1, device_id=(2 * y + (zl + j // 16) % 2, (me + j % 16) % 16),
            device_id_type=MESH,
        )
        return 0

    lax.fori_loop(1, 32, greet, 0)

    def greet_far(j, _):
        pl.semaphore_signal(
            barrier, inc=1, device_id=(2 * ((y + 1 + j // 2) % 4) + j % 2, me),
            device_id_type=MESH,
        )
        return 0

    lax.fori_loop(0, 6, greet_far, 0)

    time_rows = jnp.broadcast_to(times[...].astype(F32), (16, ROWS)).astype(BF16)

    def activate(h, _):
        for group, where in ((3, KEY), (1, VAL), (2, QUE)):
            x = 0.5 * uvqk[:, columns(group * HEADS + h)].astype(F32)
            sb[h, pl.ds(where, ROWS), :] = silu_half(x).astype(BF16)
        sb[h, pl.ds(TIM, 16), :] = time_rows
        return 0

    lax.fori_loop(0, HEADS, activate, 0)
    pl.semaphore_wait(barrier, 37)

    def m1(k):
        to = (c + k) % CHIPS
        return remote(
            sb.at[to, pl.ds(0, DNO)], rb.at[me, pl.ds(0, DNO)], m1s.at[k], m1r.at[k],
            (dp, 2 * to + r),
        )

    def m2(k):
        to = (c + k) % CHIPS
        return remote(
            sb.at[to, pl.ds(DNO, ROWS)], rb.at[me, pl.ds(DNO, ROWS)], m2s.at[k], m2r.at[k],
            (dp, 2 * to + r),
        )

    own_fw = remote(
        sb.at[c, pl.ds(0, QUE)], rb.at[me, pl.ds(0, QUE)], fws.at[0], fwr.at[0], (dp, sib)
    )

    def fw(k):
        block = 2 * ((c + CHIPS - k) % CHIPS) + r
        return remote(
            rb.at[block, pl.ds(0, QUE)], rb.at[block, pl.ds(0, QUE)], fws.at[k], fwr.at[k],
            (dp, sib),
        )

    cot_copy = remote(cot, cot2.at[pl.ds(ROWS, ROWS)], sib_s.at[0], sib_r.at[0], (dp, sib))

    for k in range(1, CHIPS):
        m1(k).start()
    own_fw.start()
    cot_copy.start()
    own1 = pltpu.make_async_copy(
        sb.at[c, pl.ds(0, DNO)], rb.at[me, pl.ds(0, DNO)], loc_sem.at[0]
    )
    own1.start()

    dh[...] = dot(cot[...], wout[...], NT)

    def d_normed(h, _):
        x = 0.5 * uvqk[:, columns(h)].astype(F32)
        u = silu_half(x).astype(BF16).astype(F32)
        sb[h, pl.ds(DNO, ROWS), :] = (dh[:, columns(h)] * u).astype(BF16)
        return 0

    lax.fori_loop(0, HEADS, d_normed, 0)
    for k in range(1, CHIPS):
        m2(k).start()
    own2 = pltpu.make_async_copy(
        sb.at[c, pl.ds(DNO, ROWS)], rb.at[me, pl.ds(DNO, ROWS)], loc_sem.at[1]
    )
    own2.start()

    cot2[pl.ds(0, ROWS), :] = cot[...]
    kext[pl.ds(0, PAD * ROWS), :] = jnp.zeros((PAD * ROWS, 2 * ROWS), BF16)
    vall[pl.ds(0, PAD * ROWS), :] = jnp.zeros((PAD * ROWS, ROWS), BF16)
    dkv[...] = jnp.zeros_like(dkv)
    pacc[...] = jnp.zeros_like(pacc)
    tmat[...] = jnp.zeros_like(tmat)
    gacc[...] = jnp.zeros_like(gacc)
    diag[...] = jnp.zeros_like(diag)
    gcol[...] = jnp.transpose(jnp.broadcast_to(gain[:, columns(c)], (ROWS, ROWS)))

    sub = lax.broadcasted_iota(jnp.int32, (ROWS, ROWS), 0)
    lane = lax.broadcasted_iota(jnp.int32, (ROWS, ROWS), 1)
    sub_s = lax.broadcasted_iota(jnp.int32, (BUCKETS, ROWS), 0)
    lane_s = lax.broadcasted_iota(jnp.int32, (BUCKETS, ROWS), 1)
    spread = jnp.abs(sub_s - lane_s % BUCKETS)
    table = jnp.zeros((BUCKETS, ROWS), F32)
    for b in range(BUCKETS):
        table = jnp.where(spread == b, ttab[c, b] * (1.0 / SCALE), table)
    part = table.astype(BF16).astype(F32)
    rest = table - part
    middle = rest.astype(BF16).astype(F32)
    table = jnp.where(
        lane_s < 16, part, jnp.where(lane_s < 32, middle, jnp.where(lane_s < 48, rest - middle, 0.0))
    )
    wa[...] = jnp.where(
        (sub >= 48) & (sub < 56) & (lane >= 48) & (lane < 56) & (sub != lane), -FAR, 0.0
    ).astype(BF16)
    wa[pl.ds(0, BUCKETS), :] = table.astype(BF16)

    for w in range(SPAN):
        gap = PAD * ROWS - w * ROWS + sub - lane
        bucket = jnp.minimum(jnp.maximum(gap, 0) // 64, BUCKETS - 1)
        tile = jnp.zeros((ROWS, ROWS), F32)
        low = 2 * (PAD - w) - 2
        for b in range(max(low, 0), min(low + 4, BUCKETS)):
            tile = jnp.where(bucket == b, 0.5 * ptab[c, b], tile)
        if low + 3 >= BUCKETS:
            tile = jnp.where(bucket == BUCKETS - 1, 0.5 * ptab[c, BUCKETS - 1], tile)
        if w == SPAN - 1:
            tile = jnp.where(gap < 0, -4096.0, tile)
        pbias[:, pl.ds(w * ROWS, ROWS)] = tile

    for k in range(1, CHIPS):
        m1(k).wait_recv()
        fw(k).start()
    own1.wait()
    own_fw.wait_recv()
    for k in range(1, CHIPS):
        fw(k).wait_recv()

    ends = [lens[0, 0]]
    for k in range(1, 7):
        ends.append(ends[-1] + lens[0, k])

    def features(block, _):
        t = rb[block, pl.ds(TIM, 16), :].astype(F32)[0:1, :]
        where = block * ROWS + lax.broadcasted_iota(jnp.int32, (1, ROWS), 1)
        user = jnp.zeros((1, ROWS), jnp.int32)
        for end in ends:
            user = user + (where >= end).astype(jnp.int32)
        index = jnp.where(sub < 48, sub % BUCKETS, sub - 48)
        value = jnp.where(sub < 48, t.astype(jnp.int32), jnp.where(sub < 56, user, -1))
        hot = jnp.where(index == value, 1.0, 0.0)
        at = pl.ds(pl.multiple_of((block + PAD) * ROWS, ROWS), ROWS)
        kext[at, pl.ds(ROWS, ROWS)] = jnp.transpose(hot).astype(BF16)
        kext[at, pl.ds(0, ROWS)] = rb[block, pl.ds(KEY, ROWS), :]
        vall[at, :] = rb[block, pl.ds(VAL, ROWS), :]
        return 0

    lax.fori_loop(0, 2 * CHIPS, features, 0)

    for k in range(1, CHIPS):
        m2(k).wait_recv()
    own2.wait()

    def att_copy(k):
        t = (c + k) % CHIPS
        return remote(att_s.at[t], att_r.at[c], ats.at[k], atr.at[k], (dp, 2 * t + r))

    def window(b, first, size):
        return pl.ds(pl.multiple_of(b * ROWS + first, ROWS), size)

    def forward(k, _):
        t = (c + k) % CHIPS
        b = 2 * t + r
        own = pl.ds(pl.multiple_of((b + PAD) * ROWS, ROWS), ROWS)
        feat = dot(kext[own, pl.ds(ROWS, ROWS)], wa[...]).astype(BF16)
        query = jnp.concatenate([rb[b, pl.ds(QUE, ROWS), :], feat], axis=1)
        total = jnp.zeros((ROWS, ROWS), F32)
        for first, size in CHUNKS:
            x = dot(query, kext[window(b, first, size), :], NT) * (0.5 * SCALE)
            x = x + pbias[:, pl.ds(first, size)]
            th = jnp.tanh(x)
            a = 1.0 + th
            w = x * a
            fsave[t, :, pl.ds(first, size)] = a + w * (1.0 - th)
            w = w.astype(BF16)
            wsave[t, :, pl.ds(first, size)] = w
            total = total + dot(w, vall[window(b, first, size), :])
        att_s[t] = total.astype(BF16)

        @pl.when(k > 0)
        def _():
            att_copy(k).start()

        tr = jnp.transpose(total)
        att_t[t] = tr
        pn = jnp.transpose(rb[b, pl.ds(DNO, ROWS), :].astype(F32))
        pn_t[t] = pn
        g = pn * gcol[...]
        mean = jnp.sum(tr, axis=0, keepdims=True) * (1.0 / ROWS)
        dev = tr - mean
        row = pl.ds(t, 1)
        stats[c, 0, row, :] = mean
        stats[c, 1, row, :] = jnp.sum(dev * dev, axis=0, keepdims=True)
        stats[c, 2, row, :] = jnp.sum(dev * g, axis=0, keepdims=True)
        stats[c, 3, row, :] = jnp.sum(g, axis=0, keepdims=True)
        return 0

    lax.fori_loop(0, CHIPS, forward, 0)

    def stat_copy(k):
        to = (c + k) % CHIPS
        return remote(stats.at[c], stats.at[c], sts.at[k], str_.at[k], (dp, 2 * to + r))

    def stat_recv(k):
        source = (c + CHIPS - k) % CHIPS
        return remote(
            stats.at[source], stats.at[source], sts.at[k], str_.at[k], (dp, 2 * source + r)
        )

    for k in range(1, CHIPS):
        stat_copy(k).start()
    att_r[c] = att_s[c]
    for k in range(1, CHIPS):
        stat_recv(k).wait_recv()

    mean = stats[0, 0]
    for h in range(1, HEADS):
        mean = mean + stats[h, 0]
    mean = mean * (1.0 / HEADS)
    spread2 = jnp.zeros((CHIPS, ROWS), F32)
    cross = jnp.zeros((CHIPS, ROWS), F32)
    gsum = jnp.zeros((CHIPS, ROWS), F32)
    for h in range(HEADS):
        off = stats[h, 0] - mean
        spread2 = spread2 + (stats[h, 1] + ROWS * (off * off))
        cross = cross + (stats[h, 2] + off * stats[h, 3])
        gsum = gsum + stats[h, 3]
    inv = lax.rsqrt(spread2 * (1.0 / WIDTH) + EPS)
    comb[0] = mean
    comb[1] = inv
    comb[2] = gsum * (1.0 / WIDTH)
    comb[3] = cross * inv * (1.0 / WIDTH)

    def d_attended(t, _):
        row = pl.ds(t, 1)
        inv_t = comb[1, row, :]
        xhat = (att_t[t] - comb[0, row, :]) * inv_t
        pn = pn_t[t]
        gacc[...] += pn * xhat
        d = inv_t * (pn * gcol[...] - comb[2, row, :] - xhat * comb[3, row, :])
        dout[t] = (0.5 * jnp.transpose(d)).astype(BF16)
        return 0

    lax.fori_loop(0, CHIPS, d_attended, 0)

    mine = pl.ds(c, 1)
    mean_c = jnp.transpose(jnp.broadcast_to(comb[0, mine, :], (ROWS, ROWS)))
    inv_c = jnp.transpose(jnp.broadcast_to(comb[1, mine, :], (ROWS, ROWS)))
    for k in range(1, CHIPS):
        att_copy(k).wait_recv()

    def rows_of(h, _):
        normed = (att_r[h].astype(F32) - mean_c) * inv_c * gain[:, columns(h)]
        x = 0.5 * uvqk[:, columns(h)].astype(F32)
        t = jnp.tanh(x)
        a = 1.0 + t
        s = x * a
        hidden = (normed * s.astype(BF16).astype(F32)).astype(BF16)
        hid[:, columns(h)] = hidden
        hid_s[h % 2, h // 2] = hidden
        d_u = dh[:, columns(h)] * normed
        dpre[:, columns(h)] = (d_u * (0.5 * (a + s * (1.0 - t)))).astype(BF16)
        return 0

    lax.fori_loop(0, HEADS, rows_of, 0)
    hid_copy = remote(
        hid_s.at[1 - r], hid2.at[:, pl.ds(ROWS, ROWS), :], sib_s.at[1], sib_r.at[1], (dp, sib)
    )
    hid_copy.start()
    hid2[:, pl.ds(0, ROWS), :] = hid_s[r]
    out[...] = (resid[...].astype(F32) + dot(hid[...], wout[...])).astype(BF16)
    cot_copy.wait_recv()
    hid_copy.wait_recv()

    def d1(k):
        to = (y + k) % 4
        return remote(ds_s.at[to], ds_r.at[y], d1s.at[k], d1r.at[k], (2 * to + zl, me))

    for k in range(1, 5):
        to = (y + k) % 4
        ds_s[to] = dot(hid2[to], cot2[...], TN).astype(BF16)
        if k < 4:
            d1(k).start()

    def dq_copy(k):
        t = (c + k) % CHIPS
        return remote(mq_s.at[t], mq_r.at[c], qs.at[k], qr.at[k], (dp, 2 * t + r))

    def backward(k, _):
        t = (c + k) % CHIPS
        b = 2 * t + r
        d = dout[t]
        diag[pl.ds(0, ROWS), pl.ds(0, ROWS)] = rb[b, pl.ds(QUE, ROWS), :]
        diag[pl.ds(ROWS, ROWS), pl.ds(ROWS, ROWS)] = d
        both = diag[...]
        dq = jnp.zeros((ROWS, 2 * ROWS), F32)
        for first, size in CHUNKS:
            at = window(b, first, size)
            some = pl.ds(first, size)
            ds = dot(d, vall[at, :], NT) * fsave[t, :, some]
            pacc[:, some] += ds
            ds = ds.astype(BF16)
            dq = dq + dot(ds, kext[at, :])
            dkv[at, :] += dot(jnp.concatenate([ds, wsave[t, :, some]], axis=0), both, TN)
        mq_s[t] = (dq[:, :ROWS] * SCALE).astype(BF16)

        @pl.when(k > 0)
        def _():
            dq_copy(k).start()

        high = dq[:, ROWS:].astype(BF16)
        low = (dq[:, ROWS:] - high.astype(F32)).astype(BF16)
        own = pl.ds(pl.multiple_of((b + PAD) * ROWS, ROWS), ROWS)
        hot = kext[own, pl.ds(ROWS, ROWS)]
        tmat[...] += dot(hot, high, TN) + dot(hot, low, TN)
        return 0

    lax.fori_loop(0, CHIPS, backward, 0)

    def to_sibling(t, _):
        at = pl.ds(pl.multiple_of((2 * t + (1 - r) + PAD) * ROWS, ROWS), ROWS)
        xs[t] = dkv[at, :].astype(BF16)
        return 0

    lax.fori_loop(0, CHIPS, to_sibling, 0)
    dkv_copy = remote(xs, xr, sib_s.at[2], sib_r.at[2], (dp, sib))
    dkv_copy.start()

    sums = []
    for b in range(BUCKETS):
        total = jnp.zeros((1, ROWS), F32)
        for w in range(SPAN):
            low = 2 * (PAD - w) - 2
            if low <= b < low + 4 or (b == BUCKETS - 1 and low + 3 >= BUCKETS):
                gap = PAD * ROWS - w * ROWS + sub - lane
                bucket = jnp.minimum(jnp.maximum(gap, 0) // 64, BUCKETS - 1)
                picked = jnp.where(bucket == b, pacc[:, pl.ds(w * ROWS, ROWS)], 0.0)
                total = total + jnp.sum(picked, axis=0, keepdims=True)
        sums.append(total)
    near = tmat[pl.ds(0, BUCKETS), :]
    gap_t = jnp.where(lane_s < BUCKETS, jnp.abs(sub_s - lane_s), -1)
    for b in range(BUCKETS):
        sums.append(jnp.sum(jnp.where(gap_t == b, near, 0.0), axis=0, keepdims=True))
    ones = jnp.ones((8, ROWS), F32)
    sums = jnp.concatenate(sums + [jnp.zeros((ROWS - 2 * BUCKETS, ROWS), F32)], axis=0)
    table_sums = exact_dot(ones, sums, NT)
    gain_sums = exact_dot(ones, gacc[...], NT)
    sub8 = lax.broadcasted_iota(jnp.int32, (8, ROWS), 0)
    tab1[dp] = jnp.where(sub8 == 0, gain_sums, table_sums)

    def t1(k):
        return remote(tab1.at[dp], tab1.at[dp], t1s.at[k], t1r.at[k], ((dp + k) % 8, me))

    def t1_recv(k):
        source = (dp + 8 - k) % 8
        return remote(tab1.at[source], tab1.at[source], t1s.at[k], t1r.at[k], (source, me))

    for k in range(1, 8):
        t1(k).start()

    dkv_copy.wait_recv()

    def kv_copy(k):
        t = (c + k) % CHIPS
        return remote(mk_s.at[t], mk_r.at[c], ks.at[k], kr.at[k], (dp, 2 * t + r))

    def join(k, _):
        t = (c + k) % CHIPS
        at = pl.ds(pl.multiple_of((2 * t + r + PAD) * ROWS, ROWS), ROWS)
        total = dkv[at, :] + xr[t].astype(F32)
        mk_s[t, 0] = (total[:, :ROWS] * SCALE).astype(BF16)
        mk_s[t, 1] = (total[:, ROWS:] * 2.0).astype(BF16)

        @pl.when(k > 0)
        def _():
            kv_copy(k).start()

        return 0

    lax.fori_loop(0, CHIPS, join, 0)
    mq_r[c] = mq_s[c]
    mk_r[c] = mk_s[c]

    for k in range(1, 4):
        d1(k).wait_recv()
    ds_r[y] = ds_s[y]
    for pair in range(CHIPS):
        at = pl.ds(pair * 16, 16)
        total = ds_r[0, at, :].astype(F32)
        for k in range(1, 4):
            total = total + ds_r[k, at, :].astype(F32)
        e_s[2 * pair] = total[:8]
        e_s[2 * pair + 1] = total[8:]

    slot = zl * CHIPS + c

    def d2(j):
        to = (me + j) % 16
        return remote(e_s.at[to], e_r.at[slot], d2s.at[j], d2r.at[slot], (2 * y + r, to))

    def d2_recv(j):
        z_from = (zl + j // CHIPS) % 2
        c_from = (c + j % CHIPS) % CHIPS
        here = z_from * CHIPS + c_from
        return remote(
            e_s.at[0], e_r.at[here], d2s.at[0], d2r.at[here], (2 * y + z_from, 2 * c_from + zl)
        )

    for j in range(1, 16):
        d2(j).start()

    @pl.when(r != zl)
    def _():
        d2(0).start()

    @pl.when(r == zl)
    def _():
        e_r[slot] = e_s[me]

    for k in range(1, 8):
        t1_recv(k).wait_recv()
    total = tab1[0]
    for k in range(1, 8):
        total = total + tab1[k]
    tab2[me] = total

    def t2(k):
        return remote(tab2.at[me], tab2.at[me], t2s.at[k], t2r.at[k], (dp, (me + k) % 16))

    def t2_recv(k):
        source = (me + 16 - k) % 16
        return remote(tab2.at[source], tab2.at[source], t2s.at[k], t2r.at[k], (dp, source))

    for k in range(1, 16):
        t2(k).start()

    for k in range(1, CHIPS):
        dq_copy(k).wait_recv()
    for k in range(1, CHIPS):
        kv_copy(k).wait_recv()

    def finish(h, _):
        for group, value in ((1, mk_r[h, 1]), (2, mq_r[h]), (3, mk_r[h, 0])):
            at = columns(group * HEADS + h)
            x = 0.5 * uvqk[:, at].astype(F32)
            dpre[:, at] = (value.astype(F32) * silu_grad_half(x)).astype(BF16)
        return 0

    lax.fori_loop(0, HEADS, finish, 0)

    for k in range(1, 16):
        t2_recv(k).wait_recv()
    for h in range(HEADS):
        pair = tab2[2 * h] + tab2[2 * h + 1]
        dgain[:, pl.ds(h * ROWS, ROWS)] = pair[0:1]
        dpos[pl.ds(h, 1), :] = pair[1:2, :BUCKETS]
        dtime[pl.ds(h, 1), :] = pair[1:2, BUCKETS : 2 * BUCKETS]

    for j in range(1, 16):
        d2_recv(j).wait_recv()

    @pl.when(r != zl)
    def _():
        d2_recv(0).wait_recv()
        d2(0).wait_send()

    total = e_r[0]
    for k in range(1, 16):
        total = total + e_r[k]
    dwo[...] = total

    own_fw.wait_send()
    cot_copy.wait_send()
    hid_copy.wait_send()
    dkv_copy.wait_send()
    for k in range(1, CHIPS):
        m1(k).wait_send()
        m2(k).wait_send()
        fw(k).wait_send()
        att_copy(k).wait_send()
        stat_copy(k).wait_send()
        dq_copy(k).wait_send()
        kv_copy(k).wait_send()
        t1(k).wait_send()
    for k in range(1, 4):
        d1(k).wait_send()
    for k in range(1, 16):
        d2(k).wait_send()
        t2(k).wait_send()


def body(
    uvqk, residual, lengths, time_buckets, pos_table, time_table, output_norm_gain, w_out, cotangent
):
    vm = pl.BlockSpec(memory_space=pltpu.VMEM)
    sm = pl.BlockSpec(memory_space=pltpu.SMEM)
    tile = (ROWS, ROWS)
    dma = pltpu.SemaphoreType.DMA
    padded = (2 * CHIPS + PAD) * ROWS
    scratch = [
        pltpu.VMEM((HEADS, END, ROWS), BF16),
        pltpu.VMEM((2 * CHIPS, END, ROWS), BF16),
        pltpu.VMEM((2 * ROWS, WIDTH), BF16),
        pltpu.VMEM((ROWS, WIDTH), F32),
        pltpu.VMEM((padded, 2 * ROWS), BF16),
        pltpu.VMEM((padded, ROWS), BF16),
        pltpu.VMEM(tile, BF16),
        pltpu.VMEM(tile, BF16),
        pltpu.VMEM((ROWS, WIN), F32),
        pltpu.VMEM((CHIPS, ROWS, WIN), BF16),
        pltpu.VMEM((CHIPS, ROWS, WIN), F32),
        pltpu.VMEM((CHIPS,) + tile, F32),
        pltpu.VMEM((CHIPS,) + tile, F32),
        pltpu.VMEM(tile, F32),
        pltpu.VMEM((CHIPS,) + tile, BF16),
        pltpu.VMEM((HEADS,) + tile, BF16),
        pltpu.VMEM((HEADS, 4, CHIPS, ROWS), F32),
        pltpu.VMEM((4, CHIPS, ROWS), F32),
        pltpu.VMEM((CHIPS,) + tile, BF16),
        pltpu.VMEM((ROWS, WIDTH), BF16),
        pltpu.VMEM((2, 4) + tile, BF16),
        pltpu.VMEM((4, 2 * ROWS, ROWS), BF16),
        pltpu.VMEM((4, ROWS, WIDTH), BF16),
        pltpu.VMEM((4, ROWS, WIDTH), BF16),
        pltpu.VMEM((16, 8, WIDTH), F32),
        pltpu.VMEM((16, 8, WIDTH), F32),
        pltpu.VMEM((2 * ROWS, 2 * ROWS), BF16),
        pltpu.VMEM((padded, 2 * ROWS), F32),
        pltpu.VMEM((ROWS, WIN), F32),
        pltpu.VMEM(tile, F32),
        pltpu.VMEM(tile, F32),
        pltpu.VMEM((CHIPS,) + tile, BF16),
        pltpu.VMEM((HEADS,) + tile, BF16),
        pltpu.VMEM((CHIPS, ROWS, 2 * ROWS), BF16),
        pltpu.VMEM((CHIPS, ROWS, 2 * ROWS), BF16),
        pltpu.VMEM((CHIPS, 2) + tile, BF16),
        pltpu.VMEM((HEADS, 2) + tile, BF16),
        pltpu.VMEM((8, ROWS), F32),
        pltpu.VMEM((8, 8, ROWS), F32),
        pltpu.VMEM((16, 8, ROWS), F32),
        dma((2,)),
    ] + [
        dma((count,))
        for count in (8, 8, 8, 8, 8, 8, 3, 3, 8, 8, 8, 8, 4, 4, 16, 16, 8, 8, 8, 8, 8, 8, 16, 16)
    ]
    out, dpre, dwo, dgain, dpos, dtime = pl.pallas_call(
        kernel,
        out_shape=(
            jax.ShapeDtypeStruct((ROWS, WIDTH), BF16),
            jax.ShapeDtypeStruct((ROWS, 4 * WIDTH), BF16),
            jax.ShapeDtypeStruct((8, WIDTH), F32),
            jax.ShapeDtypeStruct((1, WIDTH), F32),
            jax.ShapeDtypeStruct((HEADS, BUCKETS), F32),
            jax.ShapeDtypeStruct((HEADS, BUCKETS), F32),
        ),
        in_specs=[vm, vm, sm, vm, sm, sm, vm, vm, vm],
        out_specs=(vm,) * 6,
        scratch_shapes=scratch,
        compiler_params=pltpu.CompilerParams(
            collective_id=0, has_side_effects=True, vmem_limit_bytes=56 * 1024 * 1024
        ),
    )(
        uvqk[0], residual[0], lengths, time_buckets, pos_table, time_table,
        output_norm_gain[None], w_out, cotangent[0],
    )
    return (out[None], dpre[None], dwo, dgain[0], dpos, dtime)


def solution(mesh):
    in_specs = (
        P("dp", "ctx", None),
        P("dp", "ctx", None),
        P("dp", None),
        P("dp", "ctx"),
        P(),
        P(),
        P(),
        P(),
        P("dp", "ctx", None),
    )
    out_specs = (P("dp", "ctx", None), P("dp", "ctx", None), P(("dp", "ctx"), None), P(), P(), P())
    return jax.shard_map(body, mesh=mesh, in_specs=in_specs, out_specs=out_specs, check_vma=False)
```

```python
import jax
import jax.numpy as jnp
from jax import lax
from jax.experimental import pallas as pl
from jax.experimental.pallas import tpu as pltpu
from jax.sharding import PartitionSpec as P

MESH = pl.DeviceIdType.MESH
F32 = jnp.float32
BF16 = jnp.bfloat16

HEADS = 8
EPS = 1e-05
ROWS = 128
CHIPS = 8
SPAN = 9
WIN = SPAN * ROWS
PAD = SPAN - 1
WIDTH = HEADS * ROWS
BUCKETS = 16
FAR = 131072.0
SCALE = ROWS ** (-0.5)

KEY, TIM, QUE, VAL, DNO, END = 0, 128, 144, 272, 400, 528
CHUNKS = [(0, 256), (256, 256), (512, 256), (768, 256), (1024, 128)]

NT = (((1,), (1,)), ((), ()))
TN = (((0,), (0,)), ((), ()))
NN = (((1,), (0,)), ((), ()))


def dot(a, b, dims=NN):
    return lax.dot_general(a, b, dims, preferred_element_type=F32)


def exact_dot(a, b, dims=NN):
    return lax.dot_general(
        a, b, dims, preferred_element_type=F32, precision=lax.Precision.HIGHEST
    )


def silu_half(x):
    return x * (1.0 + jnp.tanh(x))


def silu_grad_half(x):
    t = jnp.tanh(x)
    a = 1.0 + t
    return 0.5 * (a + x * a * (1.0 - t))


def columns(h):
    return pl.ds(pl.multiple_of(h * ROWS, ROWS), ROWS)


def kernel(
    uvqk_h, resid_h, lens, times, ptab, ttab, gain, wout_h, cot_h,
    out, dpu, mq_r, mk_r, dwo, dgain, dpos, dtime,
    uvqk, resid, wout, cot8, sb, rb, dh, kext, vall, wa, pbias, wsave, fsave,
    att_t, pn_t, gcol, att_s, att_r, stats, comb, dout, hid, hid_s, hid8,
    e_s, e_r, diag, dkv, pacc, tmat, gacc, mq_s, xs, xr, mk_s, tab1, tab2,
    loc_sem, m1s, m1r, m2s, m2r, m3s, m3r, fws, fwr, fvs, fvr, sib_s, sib_r, ats, atr, sts, str_,
    cys, cyr, cfs, cfr, hs, hr, d2s, d2r, qs, qr, ks, kr, t1s, t1r, t2s, t2r,
):
    dp = lax.axis_index("dp")
    me = lax.axis_index("ctx")
    c = me // 2
    r = me % 2
    y = dp // 2
    zl = dp % 2
    sib = 2 * c + (1 - r)
    spot = 2 * y + r

    def remote(src, dst, ssem, rsem, to):
        return pltpu.make_async_remote_copy(
            src_ref=src, dst_ref=dst, send_sem=ssem, recv_sem=rsem, device_id=to,
            device_id_type=MESH,
        )

    load_uvqk = pltpu.make_async_copy(uvqk_h, uvqk, loc_sem.at[0])
    load_cot = pltpu.make_async_copy(cot_h, cot8.at[spot], loc_sem.at[1])
    load_wout = pltpu.make_async_copy(wout_h, wout, loc_sem.at[2])
    load_resid = pltpu.make_async_copy(resid_h, resid, loc_sem.at[3])
    load_uvqk.start()
    load_cot.start()
    load_wout.start()
    load_resid.start()

    barrier = pltpu.get_barrier_semaphore()

    def greet(j, _):
        pl.semaphore_signal(
            barrier, inc=1, device_id=(2 * y + (zl + j // 16) % 2, (me + j % 16) % 16),
            device_id_type=MESH,
        )
        return 0

    lax.fori_loop(1, 32, greet, 0)

    def greet_far(j, _):
        pl.semaphore_signal(
            barrier, inc=1, device_id=(2 * ((y + 1 + j // 2) % 4) + j % 2, me),
            device_id_type=MESH,
        )
        return 0

    lax.fori_loop(0, 6, greet_far, 0)

    time_rows = jnp.broadcast_to(times[...].astype(F32), (16, ROWS)).astype(BF16)

    def activate(h, _):
        for group, where in ((3, KEY), (2, QUE), (1, VAL)):
            x = 0.5 * uvqk[:, columns(group * HEADS + h)].astype(F32)
            sb[h, pl.ds(where, ROWS), :] = silu_half(x).astype(BF16)
        sb[h, pl.ds(TIM, 16), :] = time_rows
        return 0

    load_uvqk.wait()
    lax.fori_loop(0, HEADS, activate, 0)
    pl.semaphore_wait(barrier, 37)

    def block_rows(block):
        return pl.ds(pl.multiple_of((block + PAD) * ROWS, ROWS), ROWS)

    def m1(k):
        to = (c + k) % CHIPS
        return remote(
            sb.at[to, pl.ds(0, VAL)], rb.at[me, pl.ds(0, VAL)], m1s.at[k], m1r.at[k],
            (dp, 2 * to + r),
        )

    def m2(k):
        to = (c + k) % CHIPS
        return remote(
            sb.at[to, pl.ds(DNO, ROWS)], rb.at[me, pl.ds(DNO, ROWS)], m2s.at[k], m2r.at[k],
            (dp, 2 * to + r),
        )

    def m3(k):
        to = (c + k) % CHIPS
        return remote(
            sb.at[to, pl.ds(VAL, ROWS)], vall.at[block_rows(me)], m3s.at[k], m3r.at[k],
            (dp, 2 * to + r),
        )

    own_fw = remote(
        sb.at[c, pl.ds(0, QUE)], rb.at[me, pl.ds(0, QUE)], fws.at[0], fwr.at[0], (dp, sib)
    )
    own_fv = remote(
        sb.at[c, pl.ds(VAL, ROWS)], vall.at[block_rows(me)], fvs.at[0], fvr.at[0], (dp, sib)
    )

    def fw(k):
        block = 2 * ((c + CHIPS - k) % CHIPS) + r
        return remote(
            rb.at[block, pl.ds(0, QUE)], rb.at[block, pl.ds(0, QUE)], fws.at[k], fwr.at[k],
            (dp, sib),
        )

    def fv(k):
        at = block_rows(2 * ((c + CHIPS - k) % CHIPS) + r)
        return remote(vall.at[at], vall.at[at], fvs.at[k], fvr.at[k], (dp, sib))

    def cy(k):
        return remote(
            cot8.at[spot], cot8.at[spot], cys.at[k], cyr.at[k], (2 * ((y + k) % 4) + zl, me)
        )

    def cf(k):
        at = 2 * ((y + 4 - k) % 4) + r
        return remote(cot8.at[at], cot8.at[at], cfs.at[k], cfr.at[k], (dp, sib))

    for k in range(1, CHIPS):
        m1(k).start()
    own_fw.start()
    for k in range(1, CHIPS):
        m3(k).start()
    own_fv.start()
    rb[me, pl.ds(0, VAL), :] = sb[c, pl.ds(0, VAL), :]
    vall[block_rows(me), :] = sb[c, pl.ds(VAL, ROWS), :]
    load_cot.wait()
    for k in range(1, 4):
        cy(k).start()
    cf(0).start()

    load_wout.wait()
    dh[...] = dot(cot8[spot], wout[...], NT)

    def d_normed(h, _):
        x = 0.5 * uvqk[:, columns(h)].astype(F32)
        u = silu_half(x).astype(BF16).astype(F32)
        sb[h, pl.ds(DNO, ROWS), :] = (dh[:, columns(h)] * u).astype(BF16)
        return 0

    lax.fori_loop(0, HEADS, d_normed, 0)
    for k in range(1, CHIPS):
        m2(k).start()
    rb[me, pl.ds(DNO, ROWS), :] = sb[c, pl.ds(DNO, ROWS), :]

    kext[pl.ds(0, PAD * ROWS), :] = jnp.zeros((PAD * ROWS, 2 * ROWS), BF16)
    vall[pl.ds(0, PAD * ROWS), :] = jnp.zeros((PAD * ROWS, ROWS), BF16)
    dkv[...] = jnp.zeros_like(dkv)
    pacc[...] = jnp.zeros_like(pacc)
    tmat[...] = jnp.zeros_like(tmat)
    gacc[...] = jnp.zeros_like(gacc)
    diag[...] = jnp.zeros_like(diag)
    gcol[...] = jnp.transpose(jnp.broadcast_to(gain[:, columns(c)], (ROWS, ROWS)))

    sub = lax.broadcasted_iota(jnp.int32, (ROWS, ROWS), 0)
    lane = lax.broadcasted_iota(jnp.int32, (ROWS, ROWS), 1)
    sub_s = lax.broadcasted_iota(jnp.int32, (BUCKETS, ROWS), 0)
    lane_s = lax.broadcasted_iota(jnp.int32, (BUCKETS, ROWS), 1)
    spread = jnp.abs(sub_s - lane_s % BUCKETS)
    table = jnp.zeros((BUCKETS, ROWS), F32)
    for b in range(BUCKETS):
        table = jnp.where(spread == b, ttab[c, b] * (1.0 / SCALE), table)
    part = table.astype(BF16).astype(F32)
    rest = table - part
    middle = rest.astype(BF16).astype(F32)
    table = jnp.where(
        lane_s < 16, part, jnp.where(lane_s < 32, middle, jnp.where(lane_s < 48, rest - middle, 0.0))
    )
    wa[...] = jnp.where(
        (sub >= 48) & (sub < 56) & (lane >= 48) & (lane < 56) & (sub != lane), -FAR, 0.0
    ).astype(BF16)
    wa[pl.ds(0, BUCKETS), :] = table.astype(BF16)

    for w in range(SPAN):
        gap = PAD * ROWS - w * ROWS + sub - lane
        bucket = jnp.minimum(jnp.maximum(gap, 0) // 64, BUCKETS - 1)
        tile = jnp.zeros((ROWS, ROWS), F32)
        low = 2 * (PAD - w) - 2
        for b in range(max(low, 0), min(low + 4, BUCKETS)):
            tile = jnp.where(bucket == b, 0.5 * ptab[c, b], tile)
        if low + 3 >= BUCKETS:
            tile = jnp.where(bucket == BUCKETS - 1, 0.5 * ptab[c, BUCKETS - 1], tile)
        if w == SPAN - 1:
            tile = jnp.where(gap < 0, -4096.0, tile)
        pbias[:, pl.ds(w * ROWS, ROWS)] = tile

    for k in range(1, CHIPS):
        m1(k).wait_recv()
        fw(k).start()
    own_fw.wait_recv()
    for k in range(1, CHIPS):
        fw(k).wait_recv()

    ends = [lens[0, 0]]
    for k in range(1, 7):
        ends.append(ends[-1] + lens[0, k])

    def features(block, _):
        t = rb[block, pl.ds(TIM, 16), :].astype(F32)[0:1, :]
        where = block * ROWS + lax.broadcasted_iota(jnp.int32, (1, ROWS), 1)
        user = jnp.zeros((1, ROWS), jnp.int32)
        for end in ends:
            user = user + (where >= end).astype(jnp.int32)
        index = jnp.where(sub < 48, sub % BUCKETS, sub - 48)
        value = jnp.where(sub < 48, t.astype(jnp.int32), jnp.where(sub < 56, user, -1))
        hot = jnp.where(index == value, 1.0, 0.0)
        at = block_rows(block)
        kext[at, pl.ds(ROWS, ROWS)] = jnp.transpose(hot).astype(BF16)
        kext[at, pl.ds(0, ROWS)] = rb[block, pl.ds(KEY, ROWS), :]
        return 0

    lax.fori_loop(0, 2 * CHIPS, features, 0)

    def att_copy(k):
        t = (c + k) % CHIPS
        return remote(att_s.at[t], att_r.at[c], ats.at[k], atr.at[k], (dp, 2 * t + r))

    def window(b, first, size):
        return pl.ds(pl.multiple_of(b * ROWS + first, ROWS), size)

    def score(k, _):
        t = (c + k) % CHIPS
        b = 2 * t + r
        feat = dot(kext[block_rows(b), pl.ds(ROWS, ROWS)], wa[...]).astype(BF16)
        query = jnp.concatenate([rb[b, pl.ds(QUE, ROWS), :], feat], axis=1)
        for first, size in CHUNKS:
            x = dot(query, kext[window(b, first, size), :], NT) * (0.5 * SCALE)
            x = x + pbias[:, pl.ds(first, size)]
            th = jnp.tanh(x)
            a = 1.0 + th
            w = x * a
            fsave[t, :, pl.ds(first, size)] = a + w * (1.0 - th)
            wsave[t, :, pl.ds(first, size)] = w.astype(BF16)
        return 0

    lax.fori_loop(0, 5, score, 0)
    for k in range(1, CHIPS):
        m3(k).wait_recv()
        fv(k).start()
    lax.fori_loop(5, CHIPS, score, 0)
    own_fv.wait_recv()
    for k in range(1, CHIPS):
        fv(k).wait_recv()
    for k in range(1, CHIPS):
        m2(k).wait_recv()

    def attend(k, _):
        t = (c + k) % CHIPS
        b = 2 * t + r
        total = dot(wsave[t], vall[window(b, 0, WIN), :])
        att_s[t] = total.astype(BF16)

        @pl.when(k > 0)
        def _():
            att_copy(k).start()

        tr = jnp.transpose(total)
        att_t[t] = tr
        pn = jnp.transpose(rb[b, pl.ds(DNO, ROWS), :].astype(F32))
        pn_t[t] = pn
        g = pn * gcol[...]
        mean = jnp.sum(tr, axis=0, keepdims=True) * (1.0 / ROWS)
        dev = tr - mean
        row = pl.ds(t, 1)
        stats[c, 0, row, :] = mean
        stats[c, 1, row, :] = jnp.sum(dev * dev, axis=0, keepdims=True)
        stats[c, 2, row, :] = jnp.sum(dev * g, axis=0, keepdims=True)
        stats[c, 3, row, :] = jnp.sum(g, axis=0, keepdims=True)
        return 0

    lax.fori_loop(0, CHIPS, attend, 0)

    def stat_copy(k):
        to = (c + k) % CHIPS
        return remote(stats.at[c], stats.at[c], sts.at[k], str_.at[k], (dp, 2 * to + r))

    def stat_recv(k):
        source = (c + CHIPS - k) % CHIPS
        return remote(
            stats.at[source], stats.at[source], sts.at[k], str_.at[k], (dp, 2 * source + r)
        )

    for k in range(1, CHIPS):
        stat_copy(k).start()
    att_r[c] = att_s[c]
    for k in range(1, 4):
        cy(k).wait_recv()
        cf(k).start()
    for k in range(1, CHIPS):
        stat_recv(k).wait_recv()

    mean = stats[0, 0]
    for h in range(1, HEADS):
        mean = mean + stats[h, 0]
    mean = mean * (1.0 / HEADS)
    spread2 = jnp.zeros((CHIPS, ROWS), F32)
    cross = jnp.zeros((CHIPS, ROWS), F32)
    gsum = jnp.zeros((CHIPS, ROWS), F32)
    for h in range(HEADS):
        off = stats[h, 0] - mean
        spread2 = spread2 + (stats[h, 1] + ROWS * (off * off))
        cross = cross + (stats[h, 2] + off * stats[h, 3])
        gsum = gsum + stats[h, 3]
    inv = lax.rsqrt(spread2 * (1.0 / WIDTH) + EPS)
    comb[0] = mean
    comb[1] = inv
    comb[2] = gsum * (1.0 / WIDTH)
    comb[3] = cross * inv * (1.0 / WIDTH)

    def d_attended(t, _):
        row = pl.ds(t, 1)
        inv_t = comb[1, row, :]
        xhat = (att_t[t] - comb[0, row, :]) * inv_t
        pn = pn_t[t]
        gacc[...] += pn * xhat
        d = inv_t * (pn * gcol[...] - comb[2, row, :] - xhat * comb[3, row, :])
        dout[t] = (0.5 * jnp.transpose(d)).astype(BF16)
        return 0

    lax.fori_loop(0, CHIPS, d_attended, 0)

    mine = pl.ds(c, 1)
    mean_c = jnp.transpose(jnp.broadcast_to(comb[0, mine, :], (ROWS, ROWS)))
    inv_c = jnp.transpose(jnp.broadcast_to(comb[1, mine, :], (ROWS, ROWS)))
    for k in range(1, CHIPS):
        att_copy(k).wait_recv()

    def rows_of(h, _):
        normed = (att_r[h].astype(F32) - mean_c) * inv_c * gain[:, columns(h)]
        x = 0.5 * uvqk[:, columns(h)].astype(F32)
        t = jnp.tanh(x)
        a = 1.0 + t
        s = x * a
        hidden = (normed * s.astype(BF16).astype(F32)).astype(BF16)
        hid[:, columns(h)] = hidden
        hid_s[h] = hidden
        d_u = dh[:, columns(h)] * normed
        dpu[:, columns(h)] = (d_u * (0.5 * (a + s * (1.0 - t)))).astype(BF16)
        return 0

    lax.fori_loop(0, HEADS, rows_of, 0)

    def hid_to(j):
        y_to = (y + j // 2) % 4
        r_to = (r + j) % 2
        return remote(
            hid_s.at[2 * y_to + r_to], hid8.at[spot], hs.at[j], hr.at[j],
            (2 * y_to + zl, 2 * c + r_to),
        )

    for j in range(1, 8):
        hid_to(j).start()
    hid8[spot] = hid_s[spot]

    def dq_copy(k):
        t = (c + k) % CHIPS
        return remote(mq_s.at[t], mq_r.at[c], qs.at[k], qr.at[k], (dp, 2 * t + r))

    def backward(k, _):
        t = (c + k) % CHIPS
        b = 2 * t + r
        d = dout[t]
        diag[pl.ds(0, ROWS), pl.ds(0, ROWS)] = rb[b, pl.ds(QUE, ROWS), :]
        diag[pl.ds(ROWS, ROWS), pl.ds(ROWS, ROWS)] = d
        both = diag[...]
        dq = jnp.zeros((ROWS, 2 * ROWS), F32)
        for first, size in CHUNKS:
            at = window(b, first, size)
            some = pl.ds(first, size)
            ds = dot(d, vall[at, :], NT) * fsave[t, :, some]
            pacc[:, some] += ds
            ds = ds.astype(BF16)
            dq = dq + dot(ds, kext[at, :])
            dkv[at, :] += dot(jnp.concatenate([ds, wsave[t, :, some]], axis=0), both, TN)
        mq_s[t] = (dq[:, :ROWS] * SCALE).astype(BF16)

        @pl.when(k > 0)
        def _():
            dq_copy(k).start()

        high = dq[:, ROWS:].astype(BF16)
        low = (dq[:, ROWS:] - high.astype(F32)).astype(BF16)
        hot = kext[block_rows(b), pl.ds(ROWS, ROWS)]
        tmat[...] += dot(hot, high, TN) + dot(hot, low, TN)
        return 0

    lax.fori_loop(0, 4, backward, 0)

    for j in range(1, 8):
        hid_to(j).wait_recv()
    for k in range(4):
        cf(k).wait_recv()
    left = hid8[...].reshape(8 * ROWS, ROWS)
    for first in range(0, WIDTH, 256):
        some = pl.ds(first, 256)
        total = dot(left, cot8[:, :, some].reshape(8 * ROWS, 256), TN)
        e_s[:, :, some] = total.reshape(16, 8, 256)

    slot = zl * CHIPS + c

    def d2(j):
        to = (me + j) % 16
        return remote(e_s.at[to], e_r.at[slot], d2s.at[j], d2r.at[slot], (2 * y + r, to))

    def d2_recv(j):
        z_from = (zl + j // CHIPS) % 2
        c_from = (c + j % CHIPS) % CHIPS
        here = z_from * CHIPS + c_from
        return remote(
            e_s.at[0], e_r.at[here], d2s.at[0], d2r.at[here], (2 * y + z_from, 2 * c_from + zl)
        )

    for j in range(1, 16):
        d2(j).start()

    @pl.when(r != zl)
    def _():
        d2(0).start()

    @pl.when(r == zl)
    def _():
        e_r[slot] = e_s[me]

    lax.fori_loop(4, CHIPS, backward, 0)

    def to_sibling(t, _):
        at = pl.ds(pl.multiple_of((2 * t + (1 - r) + PAD) * ROWS, ROWS), ROWS)
        xs[t] = dkv[at, :].astype(BF16)
        return 0

    lax.fori_loop(0, CHIPS, to_sibling, 0)
    dkv_copy = remote(xs, xr, sib_s.at[0], sib_r.at[0], (dp, sib))
    dkv_copy.start()

    sums = []
    for b in range(BUCKETS):
        total = jnp.zeros((1, ROWS), F32)
        for w in range(SPAN):
            low = 2 * (PAD - w) - 2
            if low <= b < low + 4 or (b == BUCKETS - 1 and low + 3 >= BUCKETS):
                gap = PAD * ROWS - w * ROWS + sub - lane
                bucket = jnp.minimum(jnp.maximum(gap, 0) // 64, BUCKETS - 1)
                picked = jnp.where(bucket == b, pacc[:, pl.ds(w * ROWS, ROWS)], 0.0)
                total = total + jnp.sum(picked, axis=0, keepdims=True)
        sums.append(total)
    near = tmat[pl.ds(0, BUCKETS), :]
    gap_t = jnp.where(lane_s < BUCKETS, jnp.abs(sub_s - lane_s), -1)
    for b in range(BUCKETS):
        sums.append(jnp.sum(jnp.where(gap_t == b, near, 0.0), axis=0, keepdims=True))
    ones = jnp.ones((8, ROWS), F32)
    sums = jnp.concatenate(sums + [jnp.zeros((ROWS - 2 * BUCKETS, ROWS), F32)], axis=0)
    table_sums = exact_dot(ones, sums, NT)
    gain_sums = exact_dot(ones, gacc[...], NT)
    sub8 = lax.broadcasted_iota(jnp.int32, (8, ROWS), 0)
    tab1[dp] = jnp.where(sub8 == 0, gain_sums, table_sums)

    def t1(k):
        return remote(tab1.at[dp], tab1.at[dp], t1s.at[k], t1r.at[k], ((dp + k) % 8, me))

    def t1_recv(k):
        source = (dp + 8 - k) % 8
        return remote(tab1.at[source], tab1.at[source], t1s.at[k], t1r.at[k], (source, me))

    for k in range(1, 8):
        t1(k).start()

    dkv_copy.wait_recv()

    def kv_copy(k):
        t = (c + k) % CHIPS
        return remote(mk_s.at[t], mk_r.at[c], ks.at[k], kr.at[k], (dp, 2 * t + r))

    def join(k, _):
        t = (c + k) % CHIPS
        at = pl.ds(pl.multiple_of((2 * t + r + PAD) * ROWS, ROWS), ROWS)
        total = dkv[at, :] + xr[t].astype(F32)
        mk_s[t, 0] = (total[:, :ROWS] * SCALE).astype(BF16)
        mk_s[t, 1] = (total[:, ROWS:] * 2.0).astype(BF16)

        @pl.when(k > 0)
        def _():
            kv_copy(k).start()

        return 0

    lax.fori_loop(0, CHIPS, join, 0)
    mq_r[c] = mq_s[c]
    mk_r[c] = mk_s[c]
    load_resid.wait()
    out[...] = (resid[...].astype(F32) + dot(hid[...], wout[...])).astype(BF16)

    for k in range(1, 8):
        t1_recv(k).wait_recv()
    total = tab1[0]
    for k in range(1, 8):
        total = total + tab1[k]
    tab2[me] = total

    def t2(k):
        return remote(tab2.at[me], tab2.at[me], t2s.at[k], t2r.at[k], (dp, (me + k) % 16))

    def t2_recv(k):
        source = (me + 16 - k) % 16
        return remote(tab2.at[source], tab2.at[source], t2s.at[k], t2r.at[k], (dp, source))

    for k in range(1, 16):
        t2(k).start()

    for k in range(1, 16):
        t2_recv(k).wait_recv()
    for h in range(HEADS):
        pair = tab2[2 * h] + tab2[2 * h + 1]
        dgain[:, pl.ds(h * ROWS, ROWS)] = pair[0:1]
        dpos[pl.ds(h, 1), :] = pair[1:2, :BUCKETS]
        dtime[pl.ds(h, 1), :] = pair[1:2, BUCKETS : 2 * BUCKETS]

    for j in range(1, 16):
        d2_recv(j).wait_recv()

    @pl.when(r != zl)
    def _():
        d2_recv(0).wait_recv()
        d2(0).wait_send()

    total = e_r[0]
    for k in range(1, 16):
        total = total + e_r[k]
    dwo[...] = total

    for k in range(1, CHIPS):
        dq_copy(k).wait_recv()
    for k in range(1, CHIPS):
        kv_copy(k).wait_recv()

    own_fw.wait_send()
    own_fv.wait_send()
    dkv_copy.wait_send()
    for k in range(4):
        cf(k).wait_send()
    for k in range(1, CHIPS):
        m1(k).wait_send()
        m2(k).wait_send()
        m3(k).wait_send()
        fw(k).wait_send()
        fv(k).wait_send()
        hid_to(k).wait_send()
        att_copy(k).wait_send()
        stat_copy(k).wait_send()
        dq_copy(k).wait_send()
        kv_copy(k).wait_send()
        t1(k).wait_send()
    for k in range(1, 4):
        cy(k).wait_send()
    for k in range(1, 16):
        d2(k).wait_send()
        t2(k).wait_send()


def finish(uvqk, out_k, dpu, dq, dkv, dwo_k, dgain_k, dpos_k, dtime_k,
           out, dpre, dwo, dgain, dpos, dtime):
    out[...] = out_k[...]
    dpre[:, pl.ds(0, WIDTH)] = dpu[...]
    for h in range(HEADS):
        for group, value in ((1, dkv[h, 1]), (2, dq[h]), (3, dkv[h, 0])):
            at = pl.ds((group * HEADS + h) * ROWS, ROWS)
            x = 0.5 * uvqk[:, at].astype(F32)
            dpre[:, at] = (value.astype(F32) * silu_grad_half(x)).astype(BF16)
    dwo[...] = dwo_k[...]
    dgain[...] = dgain_k[...]
    dpos[...] = dpos_k[...]
    dtime[...] = dtime_k[...]


def body(
    uvqk, residual, lengths, time_buckets, pos_table, time_table, output_norm_gain, w_out, cotangent
):
    vm = pl.BlockSpec(memory_space=pltpu.VMEM)
    sm = pl.BlockSpec(memory_space=pltpu.SMEM)
    hbm = pl.BlockSpec(memory_space=pl.ANY)
    tile = (ROWS, ROWS)
    dma = pltpu.SemaphoreType.DMA
    padded = (2 * CHIPS + PAD) * ROWS
    scratch = [
        pltpu.VMEM((ROWS, 4 * WIDTH), BF16),
        pltpu.VMEM((ROWS, WIDTH), BF16),
        pltpu.VMEM((WIDTH, WIDTH), BF16),
        pltpu.VMEM((8, ROWS, WIDTH), BF16),
        pltpu.VMEM((HEADS, END, ROWS), BF16),
        pltpu.VMEM((2 * CHIPS, END, ROWS), BF16),
        pltpu.VMEM((ROWS, WIDTH), F32),
        pltpu.VMEM((padded, 2 * ROWS), BF16),
        pltpu.VMEM((padded, ROWS), BF16),
        pltpu.VMEM(tile, BF16),
        pltpu.VMEM((ROWS, WIN), F32),
        pltpu.VMEM((CHIPS, ROWS, WIN), BF16),
        pltpu.VMEM((CHIPS, ROWS, WIN), F32),
        pltpu.VMEM((CHIPS,) + tile, F32),
        pltpu.VMEM((CHIPS,) + tile, F32),
        pltpu.VMEM(tile, F32),
        pltpu.VMEM((CHIPS,) + tile, BF16),
        pltpu.VMEM((HEADS,) + tile, BF16),
        pltpu.VMEM((HEADS, 4, CHIPS, ROWS), F32),
        pltpu.VMEM((4, CHIPS, ROWS), F32),
        pltpu.VMEM((CHIPS,) + tile, BF16),
        pltpu.VMEM((ROWS, WIDTH), BF16),
        pltpu.VMEM((8,) + tile, BF16),
        pltpu.VMEM((8,) + tile, BF16),
        pltpu.VMEM((16, 8, WIDTH), F32),
        pltpu.VMEM((16, 8, WIDTH), F32),
        pltpu.VMEM((2 * ROWS, 2 * ROWS), BF16),
        pltpu.VMEM((padded, 2 * ROWS), F32),
        pltpu.VMEM((ROWS, WIN), F32),
        pltpu.VMEM(tile, F32),
        pltpu.VMEM(tile, F32),
        pltpu.VMEM((CHIPS,) + tile, BF16),
        pltpu.VMEM((CHIPS, ROWS, 2 * ROWS), BF16),
        pltpu.VMEM((CHIPS, ROWS, 2 * ROWS), BF16),
        pltpu.VMEM((CHIPS, 2) + tile, BF16),
        pltpu.VMEM((8, 8, ROWS), F32),
        pltpu.VMEM((16, 8, ROWS), F32),
        dma((4,)),
    ] + [
        dma((count,))
        for count in (
            8, 8, 8, 8, 8, 8, 8, 8, 8, 8, 1, 1, 8, 8, 8, 8,
            4, 4, 4, 4, 8, 8, 16, 16, 8, 8, 8, 8, 8, 8, 16, 16,
        )
    ]
    partial = pl.pallas_call(
        kernel,
        out_shape=(
            jax.ShapeDtypeStruct((ROWS, WIDTH), BF16),
            jax.ShapeDtypeStruct((ROWS, WIDTH), BF16),
            jax.ShapeDtypeStruct((HEADS,) + tile, BF16),
            jax.ShapeDtypeStruct((HEADS, 2) + tile, BF16),
            jax.ShapeDtypeStruct((8, WIDTH), F32),
            jax.ShapeDtypeStruct((1, WIDTH), F32),
            jax.ShapeDtypeStruct((HEADS, BUCKETS), F32),
            jax.ShapeDtypeStruct((HEADS, BUCKETS), F32),
        ),
        in_specs=[hbm, hbm, sm, vm, sm, sm, vm, hbm, hbm],
        out_specs=(vm,) * 8,
        scratch_shapes=scratch,
        compiler_params=pltpu.CompilerParams(
            collective_id=0, has_side_effects=True, vmem_limit_bytes=63 * 1024 * 1024
        ),
    )(
        uvqk[0], residual[0], lengths, time_buckets, pos_table, time_table,
        output_norm_gain[None], w_out, cotangent[0],
    )
    steps = 4
    some = ROWS // steps

    def whole(*shape):
        return pl.BlockSpec(shape, lambda i: (0,) * len(shape))

    wide = pl.BlockSpec((some, 4 * WIDTH), lambda i: (i, 0))
    narrow = pl.BlockSpec((some, WIDTH), lambda i: (i, 0))
    small = [whole(8, WIDTH), whole(1, WIDTH), whole(HEADS, BUCKETS), whole(HEADS, BUCKETS)]
    out, dpre, dwo, dgain, dpos, dtime = pl.pallas_call(
        finish,
        grid=(steps,),
        out_shape=(
            jax.ShapeDtypeStruct((ROWS, WIDTH), BF16),
            jax.ShapeDtypeStruct((ROWS, 4 * WIDTH), BF16),
            jax.ShapeDtypeStruct((8, WIDTH), F32),
            jax.ShapeDtypeStruct((1, WIDTH), F32),
            jax.ShapeDtypeStruct((HEADS, BUCKETS), F32),
            jax.ShapeDtypeStruct((HEADS, BUCKETS), F32),
        ),
        in_specs=[
            wide, narrow, narrow,
            pl.BlockSpec((HEADS, some, ROWS), lambda i: (0, i, 0)),
            pl.BlockSpec((HEADS, 2, some, ROWS), lambda i: (0, 0, i, 0)),
        ] + small,
        out_specs=[narrow, wide] + small,
        compiler_params=pltpu.CompilerParams(vmem_limit_bytes=63 * 1024 * 1024),
    )(uvqk[0], *partial)
    return (out[None], dpre[None], dwo, dgain[0], dpos, dtime)


def solution(mesh):
    in_specs = (
        P("dp", "ctx", None),
        P("dp", "ctx", None),
        P("dp", None),
        P("dp", "ctx"),
        P(),
        P(),
        P(),
        P(),
        P("dp", "ctx", None),
    )
    out_specs = (P("dp", "ctx", None), P("dp", "ctx", None), P(("dp", "ctx"), None), P(), P(), P())
    return jax.shard_map(body, mesh=mesh, in_specs=in_specs, out_specs=out_specs, check_vma=False)
```

```python
import jax
import jax.numpy as jnp
from jax import lax
from jax.experimental import pallas as pl
from jax.experimental.pallas import tpu as pltpu
from jax.sharding import PartitionSpec as P

MESH = pl.DeviceIdType.MESH
F32 = jnp.float32
BF16 = jnp.bfloat16

HEADS = 8
EPS = 1e-05
ROWS = 128
CHIPS = 8
SPAN = 9
WIN = SPAN * ROWS
PAD = SPAN - 1
WIDTH = HEADS * ROWS
BUCKETS = 16
FAR = 131072.0
SCALE = ROWS ** (-0.5)

KEY, TIM, QUE, VAL, DNO, END = 0, 128, 144, 272, 400, 528
CHUNKS = [(0, 256), (256, 256), (512, 256), (768, 256), (1024, 128)]

NT = (((1,), (1,)), ((), ()))
TN = (((0,), (0,)), ((), ()))
NN = (((1,), (0,)), ((), ()))


def dot(a, b, dims=NN):
    return lax.dot_general(a, b, dims, preferred_element_type=F32)


def exact_dot(a, b, dims=NN):
    return lax.dot_general(
        a, b, dims, preferred_element_type=F32, precision=lax.Precision.HIGHEST
    )


def silu_half(x):
    return x * (1.0 + jnp.tanh(x))


def silu_grad_half(x):
    t = jnp.tanh(x)
    a = 1.0 + t
    return 0.5 * (a + x * a * (1.0 - t))


def columns(h):
    return pl.ds(pl.multiple_of(h * ROWS, ROWS), ROWS)


def kernel(
    uvqk_h, resid_h, lens, times, ptab, ttab, gain, wout_h, cot_h,
    out, dpu, mq_r, mk_r, dwo, dgain, dpos, dtime,
    uvqk, resid, wout, cot8, sb, rb, dh, kext, vall, wa, pbias, wsave, fsave,
    att_t, pn_t, gcol, att_s, att_r, stats, comb, dout, hid, hid_s, hid8,
    e_s, e_r, diag, dq_t, dkv, pacc, tmat, gacc, mq_s, xs, xr, mk_s, tab1, tab2,
    loc_sem, m1s, m1r, m2s, m2r, m3s, m3r, fws, fwr, fvs, fvr, sib_s, sib_r, ats, atr, sts, str_,
    cys, cyr, cfs, cfr, hs, hr, d2s, d2r, qs, qr, ks, kr, t1s, t1r, t2s, t2r,
):
    dp = lax.axis_index("dp")
    me = lax.axis_index("ctx")
    c = me // 2
    r = me % 2
    y = dp // 2
    zl = dp % 2
    sib = 2 * c + (1 - r)
    spot = 2 * y + r

    def remote(src, dst, ssem, rsem, to):
        return pltpu.make_async_remote_copy(
            src_ref=src, dst_ref=dst, send_sem=ssem, recv_sem=rsem, device_id=to,
            device_id_type=MESH,
        )

    load_uvqk = pltpu.make_async_copy(uvqk_h, uvqk, loc_sem.at[0])
    load_cot = pltpu.make_async_copy(cot_h, cot8.at[spot], loc_sem.at[1])
    load_wout = pltpu.make_async_copy(wout_h, wout, loc_sem.at[2])
    load_resid = pltpu.make_async_copy(resid_h, resid, loc_sem.at[3])
    load_uvqk.start()
    load_cot.start()
    load_wout.start()
    load_resid.start()

    barrier = pltpu.get_barrier_semaphore()

    def greet(j, _):
        pl.semaphore_signal(
            barrier, inc=1, device_id=(2 * y + (zl + j // 16) % 2, (me + j % 16) % 16),
            device_id_type=MESH,
        )
        return 0

    lax.fori_loop(1, 32, greet, 0)

    def greet_far(j, _):
        pl.semaphore_signal(
            barrier, inc=1, device_id=(2 * ((y + 1 + j // 2) % 4) + j % 2, me),
            device_id_type=MESH,
        )
        return 0

    lax.fori_loop(0, 6, greet_far, 0)

    time_rows = jnp.broadcast_to(times[...].astype(F32), (16, ROWS)).astype(BF16)

    def activate(h, _):
        for group, where in ((3, KEY), (2, QUE)):
            x = 0.5 * uvqk[:, columns(group * HEADS + h)].astype(F32)
            sb[h, pl.ds(where, ROWS), :] = silu_half(x).astype(BF16)
        sb[h, pl.ds(TIM, 16), :] = time_rows
        return 0

    load_uvqk.wait()
    lax.fori_loop(0, HEADS, activate, 0)
    pl.semaphore_wait(barrier, 37)

    def block_rows(block):
        return pl.ds(pl.multiple_of((block + PAD) * ROWS, ROWS), ROWS)

    def m1(k):
        to = (c + k) % CHIPS
        return remote(
            sb.at[to, pl.ds(0, VAL)], rb.at[me, pl.ds(0, VAL)], m1s.at[k], m1r.at[k],
            (dp, 2 * to + r),
        )

    def m2(k):
        to = (c + k) % CHIPS
        return remote(
            sb.at[to, pl.ds(DNO, ROWS)], rb.at[me, pl.ds(DNO, ROWS)], m2s.at[k], m2r.at[k],
            (dp, 2 * to + r),
        )

    def m3(k):
        to = (c + k) % CHIPS
        return remote(
            sb.at[to, pl.ds(VAL, ROWS)], vall.at[block_rows(me)], m3s.at[k], m3r.at[k],
            (dp, 2 * to + r),
        )

    own_fw = remote(
        sb.at[c, pl.ds(0, QUE)], rb.at[me, pl.ds(0, QUE)], fws.at[0], fwr.at[0], (dp, sib)
    )
    own_fv = remote(
        sb.at[c, pl.ds(VAL, ROWS)], vall.at[block_rows(me)], fvs.at[0], fvr.at[0], (dp, sib)
    )

    def fw(k):
        block = 2 * ((c + CHIPS - k) % CHIPS) + r
        return remote(
            rb.at[block, pl.ds(0, QUE)], rb.at[block, pl.ds(0, QUE)], fws.at[k], fwr.at[k],
            (dp, sib),
        )

    def fv(k):
        at = block_rows(2 * ((c + CHIPS - k) % CHIPS) + r)
        return remote(vall.at[at], vall.at[at], fvs.at[k], fvr.at[k], (dp, sib))

    def cy(k):
        return remote(
            cot8.at[spot], cot8.at[spot], cys.at[k], cyr.at[k], (2 * ((y + k) % 4) + zl, me)
        )

    def cf(k):
        at = 2 * ((y + 4 - k) % 4) + r
        return remote(cot8.at[at], cot8.at[at], cfs.at[k], cfr.at[k], (dp, sib))

    for k in range(1, CHIPS):
        m1(k).start()
    own_fw.start()

    def activate_values(h, _):
        x = 0.5 * uvqk[:, columns(HEADS + h)].astype(F32)
        sb[h, pl.ds(VAL, ROWS), :] = silu_half(x).astype(BF16)
        return 0

    lax.fori_loop(0, HEADS, activate_values, 0)
    rb[me, pl.ds(0, VAL), :] = sb[c, pl.ds(0, VAL), :]
    vall[block_rows(me), :] = sb[c, pl.ds(VAL, ROWS), :]
    load_cot.wait()
    for k in range(1, 4):
        cy(k).start()
    cf(0).start()

    load_wout.wait()
    dh[...] = dot(cot8[spot], wout[...], NT)

    def d_normed(h, _):
        x = 0.5 * uvqk[:, columns(h)].astype(F32)
        u = silu_half(x).astype(BF16).astype(F32)
        sb[h, pl.ds(DNO, ROWS), :] = (dh[:, columns(h)] * u).astype(BF16)
        return 0

    lax.fori_loop(0, HEADS, d_normed, 0)
    rb[me, pl.ds(DNO, ROWS), :] = sb[c, pl.ds(DNO, ROWS), :]

    kext[pl.ds(0, PAD * ROWS), :] = jnp.zeros((PAD * ROWS, 2 * ROWS), BF16)
    vall[pl.ds(0, PAD * ROWS), :] = jnp.zeros((PAD * ROWS, ROWS), BF16)
    dkv[...] = jnp.zeros_like(dkv)
    pacc[...] = jnp.zeros_like(pacc)
    tmat[...] = jnp.zeros_like(tmat)
    gacc[...] = jnp.zeros_like(gacc)
    diag[...] = jnp.zeros_like(diag)
    gcol[...] = jnp.transpose(jnp.broadcast_to(gain[:, columns(c)], (ROWS, ROWS)))

    sub = lax.broadcasted_iota(jnp.int32, (ROWS, ROWS), 0)
    lane = lax.broadcasted_iota(jnp.int32, (ROWS, ROWS), 1)
    sub_s = lax.broadcasted_iota(jnp.int32, (BUCKETS, ROWS), 0)
    lane_s = lax.broadcasted_iota(jnp.int32, (BUCKETS, ROWS), 1)
    spread = jnp.abs(sub_s - lane_s % BUCKETS)
    table = jnp.zeros((BUCKETS, ROWS), F32)
    for b in range(BUCKETS):
        table = jnp.where(spread == b, ttab[c, b] * (1.0 / SCALE), table)
    part = table.astype(BF16).astype(F32)
    rest = table - part
    middle = rest.astype(BF16).astype(F32)
    table = jnp.where(
        lane_s < 16, part, jnp.where(lane_s < 32, middle, jnp.where(lane_s < 48, rest - middle, 0.0))
    )
    wa[...] = jnp.where(
        (sub >= 48) & (sub < 56) & (lane >= 48) & (lane < 56) & (sub != lane), -FAR, 0.0
    ).astype(BF16)
    wa[pl.ds(0, BUCKETS), :] = table.astype(BF16)

    for w in range(SPAN):
        gap = PAD * ROWS - w * ROWS + sub - lane
        bucket = jnp.minimum(jnp.maximum(gap, 0) // 64, BUCKETS - 1)
        tile = jnp.zeros((ROWS, ROWS), F32)
        low = 2 * (PAD - w) - 2
        for b in range(max(low, 0), min(low + 4, BUCKETS)):
            tile = jnp.where(bucket == b, 0.5 * ptab[c, b], tile)
        if low + 3 >= BUCKETS:
            tile = jnp.where(bucket == BUCKETS - 1, 0.5 * ptab[c, BUCKETS - 1], tile)
        if w == SPAN - 1:
            tile = jnp.where(gap < 0, -4096.0, tile)
        pbias[:, pl.ds(w * ROWS, ROWS)] = tile

    for k in range(1, CHIPS):
        m3(k).start()
    own_fv.start()

    for k in range(1, CHIPS):
        m1(k).wait_recv()
        fw(k).start()
    own_fw.wait_recv()
    for k in range(1, CHIPS):
        fw(k).wait_recv()

    for k in range(1, CHIPS):
        m2(k).start()

    ends = [lens[0, 0]]
    for k in range(1, 7):
        ends.append(ends[-1] + lens[0, k])

    def features(block, _):
        t = rb[block, pl.ds(TIM, 16), :].astype(F32)[0:1, :]
        where = block * ROWS + lax.broadcasted_iota(jnp.int32, (1, ROWS), 1)
        user = jnp.zeros((1, ROWS), jnp.int32)
        for end in ends:
            user = user + (where >= end).astype(jnp.int32)
        index = jnp.where(sub < 48, sub % BUCKETS, sub - 48)
        value = jnp.where(sub < 48, t.astype(jnp.int32), jnp.where(sub < 56, user, -1))
        hot = jnp.where(index == value, 1.0, 0.0)
        at = block_rows(block)
        kext[at, pl.ds(ROWS, ROWS)] = jnp.transpose(hot).astype(BF16)
        kext[at, pl.ds(0, ROWS)] = rb[block, pl.ds(KEY, ROWS), :]
        return 0

    lax.fori_loop(0, 2 * CHIPS, features, 0)

    def att_copy(k):
        t = (c + k) % CHIPS
        return remote(att_s.at[t], att_r.at[c], ats.at[k], atr.at[k], (dp, 2 * t + r))

    def window(b, first, size):
        return pl.ds(pl.multiple_of(b * ROWS + first, ROWS), size)

    def for_reach(t, run):
        for reach in (2, 4, 6, SPAN):
            @pl.when((t == reach // 2 - 1) if reach < SPAN else (t >= 3))
            def _():
                run((SPAN - reach) * ROWS, reach * ROWS)

    def score(k, _):
        t = (c + k) % CHIPS
        b = 2 * t + r
        feat = dot(kext[block_rows(b), pl.ds(ROWS, ROWS)], wa[...]).astype(BF16)
        query = jnp.concatenate([rb[b, pl.ds(QUE, ROWS), :], feat], axis=1)

        def run(start, length):
            for first in range(start, WIN, 256):
                size = min(256, WIN - first)
                x = dot(query, kext[window(b, first, size), :], NT) * (0.5 * SCALE)
                x = x + pbias[:, pl.ds(first, size)]
                th = jnp.tanh(x)
                a = 1.0 + th
                w = x * a
                fsave[t, :, pl.ds(first, size)] = a + w * (1.0 - th)
                wsave[t, :, pl.ds(first, size)] = w.astype(BF16)

        for_reach(t, run)
        return 0

    lax.fori_loop(0, 5, score, 0)
    for k in range(1, CHIPS):
        m3(k).wait_recv()
        fv(k).start()
    lax.fori_loop(5, CHIPS, score, 0)
    own_fv.wait_recv()
    for k in range(1, CHIPS):
        fv(k).wait_recv()

    def attend(k, _):
        t = (c + k) % CHIPS

        def run(start, length):
            total = dot(
                wsave[t, :, pl.ds(start, length)], vall[window(2 * t + r, start, length), :]
            )
            att_s[t] = total.astype(BF16)
            att_t[t] = jnp.transpose(total)

        for_reach(t, run)
        tr = att_t[t]
        mean = jnp.sum(tr, axis=0, keepdims=True) * (1.0 / ROWS)
        dev = tr - mean
        row = pl.ds(t, 1)
        stats[c, 0, row, :] = mean
        stats[c, 1, row, :] = jnp.sum(dev * dev, axis=0, keepdims=True)
        return 0

    lax.fori_loop(0, CHIPS, attend, 0)
    for k in range(1, CHIPS):
        m2(k).wait_recv()

    def moments(t, _):
        pn = jnp.transpose(rb[2 * t + r, pl.ds(DNO, ROWS), :].astype(F32))
        pn_t[t] = pn
        g = pn * gcol[...]
        row = pl.ds(t, 1)
        dev = att_t[t] - stats[c, 0, row, :]
        stats[c, 2, row, :] = jnp.sum(dev * g, axis=0, keepdims=True)
        stats[c, 3, row, :] = jnp.sum(g, axis=0, keepdims=True)
        return 0

    lax.fori_loop(0, CHIPS, moments, 0)

    def stat_copy(k):
        to = (c + k) % CHIPS
        return remote(stats.at[c], stats.at[c], sts.at[k], str_.at[k], (dp, 2 * to + r))

    def stat_recv(k):
        source = (c + CHIPS - k) % CHIPS
        return remote(
            stats.at[source], stats.at[source], sts.at[k], str_.at[k], (dp, 2 * source + r)
        )

    for k in range(1, CHIPS):
        stat_copy(k).start()
    for k in range(1, CHIPS):
        att_copy(k).start()
    att_r[c] = att_s[c]
    for k in range(1, 4):
        cy(k).wait_recv()
        cf(k).start()
    for k in range(1, CHIPS):
        stat_recv(k).wait_recv()

    mean = stats[0, 0]
    for h in range(1, HEADS):
        mean = mean + stats[h, 0]
    mean = mean * (1.0 / HEADS)
    spread2 = jnp.zeros((CHIPS, ROWS), F32)
    cross = jnp.zeros((CHIPS, ROWS), F32)
    gsum = jnp.zeros((CHIPS, ROWS), F32)
    for h in range(HEADS):
        off = stats[h, 0] - mean
        spread2 = spread2 + (stats[h, 1] + ROWS * (off * off))
        cross = cross + (stats[h, 2] + off * stats[h, 3])
        gsum = gsum + stats[h, 3]
    inv = lax.rsqrt(spread2 * (1.0 / WIDTH) + EPS)
    comb[0] = mean
    comb[1] = inv
    comb[2] = gsum * (1.0 / WIDTH)
    comb[3] = cross * inv * (1.0 / WIDTH)

    def d_attended(t, _):
        row = pl.ds(t, 1)
        inv_t = comb[1, row, :]
        xhat = (att_t[t] - comb[0, row, :]) * inv_t
        pn = pn_t[t]
        gacc[...] += pn * xhat
        d = inv_t * (pn * gcol[...] - comb[2, row, :] - xhat * comb[3, row, :])
        dout[t] = (0.5 * jnp.transpose(d)).astype(BF16)
        return 0

    lax.fori_loop(0, CHIPS, d_attended, 0)

    def dq_copy(k):
        t = (c + k) % CHIPS
        return remote(mq_s.at[t], mq_r.at[c], qs.at[k], qr.at[k], (dp, 2 * t + r))

    def backward(k, _):
        t = (c + k) % CHIPS
        b = 2 * t + r
        d = dout[t]
        diag[pl.ds(0, ROWS), pl.ds(0, ROWS)] = rb[b, pl.ds(QUE, ROWS), :]
        diag[pl.ds(ROWS, ROWS), pl.ds(ROWS, ROWS)] = d
        both = diag[...]

        def run(start, length):
            at = window(b, start, length)
            some = pl.ds(start, length)
            ds = dot(d, vall[at, :], NT) * fsave[t, :, some]
            pacc[:, some] += ds
            ds = ds.astype(BF16)
            dq_t[...] = dot(ds, kext[at, :])
            dkv[at, :] += dot(jnp.concatenate([ds, wsave[t, :, some]], axis=0), both, TN)

        for_reach(t, run)
        dq = dq_t[...]
        mq_s[t] = (dq[:, :ROWS] * SCALE).astype(BF16)

        @pl.when(k > 0)
        def _():
            dq_copy(k).start()

        high = dq[:, ROWS:].astype(BF16)
        low = (dq[:, ROWS:] - high.astype(F32)).astype(BF16)
        hot = kext[block_rows(b), pl.ds(ROWS, ROWS)]
        tmat[...] += dot(hot, high, TN) + dot(hot, low, TN)
        return 0

    lax.fori_loop(0, 2, backward, 0)

    mine = pl.ds(c, 1)
    mean_c = jnp.transpose(jnp.broadcast_to(comb[0, mine, :], (ROWS, ROWS)))
    inv_c = jnp.transpose(jnp.broadcast_to(comb[1, mine, :], (ROWS, ROWS)))
    for k in range(1, CHIPS):
        att_copy(k).wait_recv()

    def rows_of(h, _):
        normed = (att_r[h].astype(F32) - mean_c) * inv_c * gain[:, columns(h)]
        x = 0.5 * uvqk[:, columns(h)].astype(F32)
        t = jnp.tanh(x)
        a = 1.0 + t
        s = x * a
        hidden = (normed * s.astype(BF16).astype(F32)).astype(BF16)
        hid[:, columns(h)] = hidden
        hid_s[h] = hidden
        d_u = dh[:, columns(h)] * normed
        dpu[:, columns(h)] = (d_u * (0.5 * (a + s * (1.0 - t)))).astype(BF16)
        return 0

    lax.fori_loop(0, HEADS, rows_of, 0)

    def hid_to(j):
        y_to = (y + j // 2) % 4
        r_to = (r + j) % 2
        return remote(
            hid_s.at[2 * y_to + r_to], hid8.at[spot], hs.at[j], hr.at[j],
            (2 * y_to + zl, 2 * c + r_to),
        )

    for j in range(1, 8):
        hid_to(j).start()
    hid8[spot] = hid_s[spot]

    lax.fori_loop(2, CHIPS, backward, 0)

    def to_sibling(t, _):
        at = pl.ds(pl.multiple_of((2 * t + (1 - r) + PAD) * ROWS, ROWS), ROWS)
        xs[t] = dkv[at, :].astype(BF16)
        return 0

    lax.fori_loop(0, CHIPS, to_sibling, 0)
    dkv_copy = remote(xs, xr, sib_s.at[0], sib_r.at[0], (dp, sib))
    dkv_copy.start()

    sums = []
    for b in range(BUCKETS):
        total = jnp.zeros((1, ROWS), F32)
        for w in range(SPAN):
            low = 2 * (PAD - w) - 2
            if low <= b < low + 4 or (b == BUCKETS - 1 and low + 3 >= BUCKETS):
                gap = PAD * ROWS - w * ROWS + sub - lane
                bucket = jnp.minimum(jnp.maximum(gap, 0) // 64, BUCKETS - 1)
                picked = jnp.where(bucket == b, pacc[:, pl.ds(w * ROWS, ROWS)], 0.0)
                total = total + jnp.sum(picked, axis=0, keepdims=True)
        sums.append(total)
    near = tmat[pl.ds(0, BUCKETS), :]
    gap_t = jnp.where(lane_s < BUCKETS, jnp.abs(sub_s - lane_s), -1)
    for b in range(BUCKETS):
        sums.append(jnp.sum(jnp.where(gap_t == b, near, 0.0), axis=0, keepdims=True))
    ones = jnp.ones((8, ROWS), F32)
    sums = jnp.concatenate(sums + [jnp.zeros((ROWS - 2 * BUCKETS, ROWS), F32)], axis=0)
    table_sums = exact_dot(ones, sums, NT)
    gain_sums = exact_dot(ones, gacc[...], NT)
    sub8 = lax.broadcasted_iota(jnp.int32, (8, ROWS), 0)
    tab1[dp] = jnp.where(sub8 == 0, gain_sums, table_sums)

    def t1(k):
        return remote(tab1.at[dp], tab1.at[dp], t1s.at[k], t1r.at[k], ((dp + k) % 8, me))

    def t1_recv(k):
        source = (dp + 8 - k) % 8
        return remote(tab1.at[source], tab1.at[source], t1s.at[k], t1r.at[k], (source, me))

    for k in range(1, 8):
        t1(k).start()

    for j in range(1, 8):
        hid_to(j).wait_recv()
    for k in range(4):
        cf(k).wait_recv()
    left = hid8[...].reshape(8 * ROWS, ROWS)
    for first in range(0, WIDTH // 2, 256):
        parts = [
            dot(left, cot8[:, :, pl.ds(at, 256)].reshape(8 * ROWS, 256), TN).reshape(16, 8, 256)
            for at in (first, first + WIDTH // 2)
        ]
        e_s[:, :, pl.ds(first, 256)] = jnp.concatenate(parts, axis=1).astype(BF16)

    slot = zl * CHIPS + c

    def d2(j):
        to = (me + j) % 16
        return remote(e_s.at[to], e_r.at[slot], d2s.at[j], d2r.at[slot], (2 * y + r, to))

    def d2_recv(j):
        z_from = (zl + j // CHIPS) % 2
        c_from = (c + j % CHIPS) % CHIPS
        here = z_from * CHIPS + c_from
        return remote(
            e_s.at[0], e_r.at[here], d2s.at[0], d2r.at[here], (2 * y + z_from, 2 * c_from + zl)
        )

    for j in range(1, 16):
        d2(j).start()

    @pl.when(r != zl)
    def _():
        d2(0).start()

    @pl.when(r == zl)
    def _():
        e_r[slot] = e_s[me]

    for k in range(1, 8):
        t1_recv(k).wait_recv()
    total = tab1[0]
    for k in range(1, 8):
        total = total + tab1[k]
    tab2[me] = total

    def t2(k):
        return remote(tab2.at[me], tab2.at[me], t2s.at[k], t2r.at[k], (dp, (me + k) % 16))

    def t2_recv(k):
        source = (me + 16 - k) % 16
        return remote(tab2.at[source], tab2.at[source], t2s.at[k], t2r.at[k], (dp, source))

    for k in range(1, 16):
        t2(k).start()

    dkv_copy.wait_recv()

    def kv_copy(k):
        t = (c + k) % CHIPS
        return remote(mk_s.at[t], mk_r.at[c], ks.at[k], kr.at[k], (dp, 2 * t + r))

    def join(k, _):
        t = (c + k) % CHIPS
        at = pl.ds(pl.multiple_of((2 * t + r + PAD) * ROWS, ROWS), ROWS)
        total = dkv[at, :] + xr[t].astype(F32)
        mk_s[t, 0] = (total[:, :ROWS] * SCALE).astype(BF16)
        mk_s[t, 1] = (total[:, ROWS:] * 2.0).astype(BF16)

        @pl.when(k > 0)
        def _():
            kv_copy(k).start()

        return 0

    lax.fori_loop(0, CHIPS, join, 0)
    mq_r[c] = mq_s[c]
    mk_r[c] = mk_s[c]
    load_resid.wait()
    out[...] = (resid[...].astype(F32) + dot(hid[...], wout[...])).astype(BF16)


    for k in range(1, 16):
        t2_recv(k).wait_recv()
    for h in range(HEADS):
        pair = tab2[2 * h] + tab2[2 * h + 1]
        dgain[:, pl.ds(h * ROWS, ROWS)] = pair[0:1]
        dpos[pl.ds(h, 1), :] = pair[1:2, :BUCKETS]
        dtime[pl.ds(h, 1), :] = pair[1:2, BUCKETS : 2 * BUCKETS]

    for j in range(1, 16):
        d2_recv(j).wait_recv()

    @pl.when(r != zl)
    def _():
        d2_recv(0).wait_recv()
        d2(0).wait_send()

    total = e_r[0].astype(F32)
    for k in range(1, 16):
        total = total + e_r[k].astype(F32)
    dwo[:, pl.ds(0, WIDTH // 2)] = total[:8]
    dwo[:, pl.ds(WIDTH // 2, WIDTH // 2)] = total[8:]

    for k in range(1, CHIPS):
        dq_copy(k).wait_recv()
    for k in range(1, CHIPS):
        kv_copy(k).wait_recv()

    own_fw.wait_send()
    own_fv.wait_send()
    dkv_copy.wait_send()
    for k in range(4):
        cf(k).wait_send()
    for k in range(1, CHIPS):
        m1(k).wait_send()
        m2(k).wait_send()
        m3(k).wait_send()
        fw(k).wait_send()
        fv(k).wait_send()
        hid_to(k).wait_send()
        att_copy(k).wait_send()
        stat_copy(k).wait_send()
        dq_copy(k).wait_send()
        kv_copy(k).wait_send()
        t1(k).wait_send()
    for k in range(1, 4):
        cy(k).wait_send()
    for k in range(1, 16):
        d2(k).wait_send()
        t2(k).wait_send()


def finish(uvqk, out_k, dpu, dq, dkv, dwo_k, dgain_k, dpos_k, dtime_k,
           out, dpre, dwo, dgain, dpos, dtime):
    out[...] = out_k[...]
    dpre[:, pl.ds(0, WIDTH)] = dpu[...]
    for h in range(HEADS):
        for group, value in ((1, dkv[h, 1]), (2, dq[h]), (3, dkv[h, 0])):
            at = pl.ds((group * HEADS + h) * ROWS, ROWS)
            x = 0.5 * uvqk[:, at].astype(F32)
            dpre[:, at] = (value.astype(F32) * silu_grad_half(x)).astype(BF16)
    dwo[...] = dwo_k[...]
    dgain[...] = dgain_k[...]
    dpos[...] = dpos_k[...]
    dtime[...] = dtime_k[...]


def body(
    uvqk, residual, lengths, time_buckets, pos_table, time_table, output_norm_gain, w_out, cotangent
):
    vm = pl.BlockSpec(memory_space=pltpu.VMEM)
    sm = pl.BlockSpec(memory_space=pltpu.SMEM)
    hbm = pl.BlockSpec(memory_space=pl.ANY)
    tile = (ROWS, ROWS)
    dma = pltpu.SemaphoreType.DMA
    padded = (2 * CHIPS + PAD) * ROWS
    scratch = [
        pltpu.VMEM((ROWS, 4 * WIDTH), BF16),
        pltpu.VMEM((ROWS, WIDTH), BF16),
        pltpu.VMEM((WIDTH, WIDTH), BF16),
        pltpu.VMEM((8, ROWS, WIDTH), BF16),
        pltpu.VMEM((HEADS, END, ROWS), BF16),
        pltpu.VMEM((2 * CHIPS, END, ROWS), BF16),
        pltpu.VMEM((ROWS, WIDTH), F32),
        pltpu.VMEM((padded, 2 * ROWS), BF16),
        pltpu.VMEM((padded, ROWS), BF16),
        pltpu.VMEM(tile, BF16),
        pltpu.VMEM((ROWS, WIN), F32),
        pltpu.VMEM((CHIPS, ROWS, WIN), BF16),
        pltpu.VMEM((CHIPS, ROWS, WIN), F32),
        pltpu.VMEM((CHIPS,) + tile, F32),
        pltpu.VMEM((CHIPS,) + tile, F32),
        pltpu.VMEM(tile, F32),
        pltpu.VMEM((CHIPS,) + tile, BF16),
        pltpu.VMEM((HEADS,) + tile, BF16),
        pltpu.VMEM((HEADS, 4, CHIPS, ROWS), F32),
        pltpu.VMEM((4, CHIPS, ROWS), F32),
        pltpu.VMEM((CHIPS,) + tile, BF16),
        pltpu.VMEM((ROWS, WIDTH), BF16),
        pltpu.VMEM((8,) + tile, BF16),
        pltpu.VMEM((8,) + tile, BF16),
        pltpu.VMEM((16, 16, WIDTH // 2), BF16),
        pltpu.VMEM((16, 16, WIDTH // 2), BF16),
        pltpu.VMEM((2 * ROWS, 2 * ROWS), BF16),
        pltpu.VMEM((ROWS, 2 * ROWS), F32),
        pltpu.VMEM((padded, 2 * ROWS), F32),
        pltpu.VMEM((ROWS, WIN), F32),
        pltpu.VMEM(tile, F32),
        pltpu.VMEM(tile, F32),
        pltpu.VMEM((CHIPS,) + tile, BF16),
        pltpu.VMEM((CHIPS, ROWS, 2 * ROWS), BF16),
        pltpu.VMEM((CHIPS, ROWS, 2 * ROWS), BF16),
        pltpu.VMEM((CHIPS, 2) + tile, BF16),
        pltpu.VMEM((8, 8, ROWS), F32),
        pltpu.VMEM((16, 8, ROWS), F32),
        dma((4,)),
    ] + [
        dma((count,))
        for count in (
            8, 8, 8, 8, 8, 8, 8, 8, 8, 8, 1, 1, 8, 8, 8, 8,
            4, 4, 4, 4, 8, 8, 16, 16, 8, 8, 8, 8, 8, 8, 16, 16,
        )
    ]
    partial = pl.pallas_call(
        kernel,
        out_shape=(
            jax.ShapeDtypeStruct((ROWS, WIDTH), BF16),
            jax.ShapeDtypeStruct((ROWS, WIDTH), BF16),
            jax.ShapeDtypeStruct((HEADS,) + tile, BF16),
            jax.ShapeDtypeStruct((HEADS, 2) + tile, BF16),
            jax.ShapeDtypeStruct((8, WIDTH), F32),
            jax.ShapeDtypeStruct((1, WIDTH), F32),
            jax.ShapeDtypeStruct((HEADS, BUCKETS), F32),
            jax.ShapeDtypeStruct((HEADS, BUCKETS), F32),
        ),
        in_specs=[hbm, hbm, sm, vm, sm, sm, vm, hbm, hbm],
        out_specs=(vm,) * 8,
        scratch_shapes=scratch,
        compiler_params=pltpu.CompilerParams(
            collective_id=0, has_side_effects=True, vmem_limit_bytes=63 * 1024 * 1024
        ),
    )(
        uvqk[0], residual[0], lengths, time_buckets, pos_table, time_table,
        output_norm_gain[None], w_out, cotangent[0],
    )
    steps = 2
    some = ROWS // steps

    def whole(*shape):
        return pl.BlockSpec(shape, lambda i: (0,) * len(shape))

    wide = pl.BlockSpec((some, 4 * WIDTH), lambda i: (i, 0))
    narrow = pl.BlockSpec((some, WIDTH), lambda i: (i, 0))
    small = [whole(8, WIDTH), whole(1, WIDTH), whole(HEADS, BUCKETS), whole(HEADS, BUCKETS)]
    out, dpre, dwo, dgain, dpos, dtime = pl.pallas_call(
        finish,
        grid=(steps,),
        out_shape=(
            jax.ShapeDtypeStruct((ROWS, WIDTH), BF16),
            jax.ShapeDtypeStruct((ROWS, 4 * WIDTH), BF16),
            jax.ShapeDtypeStruct((8, WIDTH), F32),
            jax.ShapeDtypeStruct((1, WIDTH), F32),
            jax.ShapeDtypeStruct((HEADS, BUCKETS), F32),
            jax.ShapeDtypeStruct((HEADS, BUCKETS), F32),
        ),
        in_specs=[
            wide, narrow, narrow,
            pl.BlockSpec((HEADS, some, ROWS), lambda i: (0, i, 0)),
            pl.BlockSpec((HEADS, 2, some, ROWS), lambda i: (0, 0, i, 0)),
        ] + small,
        out_specs=[narrow, wide] + small,
        compiler_params=pltpu.CompilerParams(vmem_limit_bytes=63 * 1024 * 1024),
    )(uvqk[0], *partial)
    return (out[None], dpre[None], dwo, dgain[0], dpos, dtime)


def solution(mesh):
    in_specs = (
        P("dp", "ctx", None),
        P("dp", "ctx", None),
        P("dp", None),
        P("dp", "ctx"),
        P(),
        P(),
        P(),
        P(),
        P("dp", "ctx", None),
    )
    out_specs = (P("dp", "ctx", None), P("dp", "ctx", None), P(("dp", "ctx"), None), P(), P(), P())
    return jax.shard_map(body, mesh=mesh, in_specs=in_specs, out_specs=out_specs, check_vma=False)
```

```python
import jax
import jax.numpy as jnp
from jax import lax
from jax.experimental import pallas as pl
from jax.experimental.pallas import tpu as pltpu
from jax.sharding import PartitionSpec as P

MESH = pl.DeviceIdType.MESH
F32 = jnp.float32
BF16 = jnp.bfloat16

HEADS = 8
EPS = 1e-05
ROWS = 128
CHIPS = 8
SPAN = 9
WIN = SPAN * ROWS
PAD = SPAN - 1
FAR_FIRST = (5, 3, 4, 7, 1, 2, 6)
WIDTH = HEADS * ROWS
BUCKETS = 16
FAR = 131072.0
SCALE = ROWS ** (-0.5)

KEY, TIM, QUE, VAL, DNO, END = 0, 128, 144, 272, 400, 528
CHUNKS = [(0, 256), (256, 256), (512, 256), (768, 256), (1024, 128)]

NT = (((1,), (1,)), ((), ()))
TN = (((0,), (0,)), ((), ()))
NN = (((1,), (0,)), ((), ()))


def dot(a, b, dims=NN):
    return lax.dot_general(a, b, dims, preferred_element_type=F32)


def exact_dot(a, b, dims=NN):
    return lax.dot_general(
        a, b, dims, preferred_element_type=F32, precision=lax.Precision.HIGHEST
    )


def silu_half(x):
    return x * (1.0 + jnp.tanh(x))


def silu_grad_half(x):
    t = jnp.tanh(x)
    a = 1.0 + t
    return 0.5 * (a + x * a * (1.0 - t))


def columns(h):
    return pl.ds(pl.multiple_of(h * ROWS, ROWS), ROWS)


def kernel(
    uvqk_h, resid_h, lens, times, ptab, ttab, gain, wout_h, cot_h,
    out, dpu, mq_r, mk_r, dwo, dgain, dpos, dtime,
    uvqk, resid, wout, cot8, sb, rb, dh, kext, vall, wa, pbias, wsave, fsave,
    att_t, pn_t, gcol, att_s, att_r, stats, comb, dout, hid, hid_s, hid8,
    e_s, e_r, diag, dq_t, dkv, pacc, tmat, gacc, mq_s, xs, xr, mk_s, tab1, tab2,
    loc_sem, m1s, m1r, m2s, m2r, m3s, m3r, fws, fwr, fvs, fvr, sib_s, sib_r, ats, atr, sts, str_,
    cys, cyr, cfs, cfr, hs, hr, d2s, d2r, qs, qr, ks, kr, t1s, t1r, t2s, t2r,
):
    dp = lax.axis_index("dp")
    me = lax.axis_index("ctx")
    c = me // 2
    r = me % 2
    y = dp // 2
    zl = dp % 2
    sib = 2 * c + (1 - r)
    spot = 2 * y + r

    def remote(src, dst, ssem, rsem, to):
        return pltpu.make_async_remote_copy(
            src_ref=src, dst_ref=dst, send_sem=ssem, recv_sem=rsem, device_id=to,
            device_id_type=MESH,
        )

    load_uvqk = pltpu.make_async_copy(uvqk_h, uvqk, loc_sem.at[0])
    load_cot = pltpu.make_async_copy(cot_h, cot8.at[spot], loc_sem.at[1])
    load_wout = pltpu.make_async_copy(wout_h, wout, loc_sem.at[2])
    load_resid = pltpu.make_async_copy(resid_h, resid, loc_sem.at[3])
    load_uvqk.start()
    load_cot.start()
    load_wout.start()
    load_resid.start()

    barrier = pltpu.get_barrier_semaphore()

    def greet(j, _):
        pl.semaphore_signal(
            barrier, inc=1, device_id=(2 * y + (zl + j // 16) % 2, (me + j % 16) % 16),
            device_id_type=MESH,
        )
        return 0

    lax.fori_loop(1, 32, greet, 0)

    def greet_far(j, _):
        pl.semaphore_signal(
            barrier, inc=1, device_id=(2 * ((y + 1 + j // 2) % 4) + j % 2, me),
            device_id_type=MESH,
        )
        return 0

    lax.fori_loop(0, 6, greet_far, 0)

    time_rows = jnp.broadcast_to(times[...].astype(F32), (16, ROWS)).astype(BF16)

    def activate(h, _):
        for group, where in ((3, KEY), (2, QUE)):
            x = 0.5 * uvqk[:, columns(group * HEADS + h)].astype(F32)
            sb[h, pl.ds(where, ROWS), :] = silu_half(x).astype(BF16)
        sb[h, pl.ds(TIM, 16), :] = time_rows
        return 0

    load_uvqk.wait()
    lax.fori_loop(0, HEADS, activate, 0)
    pl.semaphore_wait(barrier, 37)

    def block_rows(block):
        return pl.ds(pl.multiple_of((block + PAD) * ROWS, ROWS), ROWS)

    def m1(k):
        to = (c + k) % CHIPS
        return remote(
            sb.at[to, pl.ds(0, VAL)], rb.at[me, pl.ds(0, VAL)], m1s.at[k], m1r.at[k],
            (dp, 2 * to + r),
        )

    def m2(k):
        to = (c + k) % CHIPS
        return remote(
            sb.at[to, pl.ds(DNO, ROWS)], rb.at[me, pl.ds(DNO, ROWS)], m2s.at[k], m2r.at[k],
            (dp, 2 * to + r),
        )

    def m3(k):
        to = (c + k) % CHIPS
        return remote(
            sb.at[to, pl.ds(VAL, ROWS)], vall.at[block_rows(me)], m3s.at[k], m3r.at[k],
            (dp, 2 * to + r),
        )

    own_fw = remote(
        sb.at[c, pl.ds(0, QUE)], rb.at[me, pl.ds(0, QUE)], fws.at[0], fwr.at[0], (dp, sib)
    )
    own_fv = remote(
        sb.at[c, pl.ds(VAL, ROWS)], vall.at[block_rows(me)], fvs.at[0], fvr.at[0], (dp, sib)
    )

    def fw(k):
        block = 2 * ((c + CHIPS - k) % CHIPS) + r
        return remote(
            rb.at[block, pl.ds(0, QUE)], rb.at[block, pl.ds(0, QUE)], fws.at[k], fwr.at[k],
            (dp, sib),
        )

    def fv(k):
        at = block_rows(2 * ((c + CHIPS - k) % CHIPS) + r)
        return remote(vall.at[at], vall.at[at], fvs.at[k], fvr.at[k], (dp, sib))

    def cy(k):
        return remote(
            cot8.at[spot], cot8.at[spot], cys.at[k], cyr.at[k], (2 * ((y + k) % 4) + zl, me)
        )

    def cf(k):
        at = 2 * ((y + 4 - k) % 4) + r
        return remote(cot8.at[at], cot8.at[at], cfs.at[k], cfr.at[k], (dp, sib))

    for k in FAR_FIRST:
        m1(k).start()
    own_fw.start()

    def activate_values(h, _):
        x = 0.5 * uvqk[:, columns(HEADS + h)].astype(F32)
        sb[h, pl.ds(VAL, ROWS), :] = silu_half(x).astype(BF16)
        return 0

    lax.fori_loop(0, HEADS, activate_values, 0)
    rb[me, pl.ds(0, VAL), :] = sb[c, pl.ds(0, VAL), :]
    vall[block_rows(me), :] = sb[c, pl.ds(VAL, ROWS), :]
    load_cot.wait()
    for k in range(1, 4):
        cy(k).start()
    cf(0).start()

    load_wout.wait()
    dh[...] = dot(cot8[spot], wout[...], NT)

    def d_normed(h, _):
        x = 0.5 * uvqk[:, columns(h)].astype(F32)
        u = silu_half(x).astype(BF16).astype(F32)
        sb[h, pl.ds(DNO, ROWS), :] = (dh[:, columns(h)] * u).astype(BF16)
        return 0

    lax.fori_loop(0, HEADS, d_normed, 0)
    rb[me, pl.ds(DNO, ROWS), :] = sb[c, pl.ds(DNO, ROWS), :]

    kext[pl.ds(0, PAD * ROWS), :] = jnp.zeros((PAD * ROWS, 2 * ROWS), BF16)
    vall[pl.ds(0, PAD * ROWS), :] = jnp.zeros((PAD * ROWS, ROWS), BF16)
    dkv[...] = jnp.zeros_like(dkv)
    pacc[...] = jnp.zeros_like(pacc)
    tmat[...] = jnp.zeros_like(tmat)
    gacc[...] = jnp.zeros_like(gacc)
    diag[...] = jnp.zeros_like(diag)
    gcol[...] = jnp.transpose(jnp.broadcast_to(gain[:, columns(c)], (ROWS, ROWS)))

    sub = lax.broadcasted_iota(jnp.int32, (ROWS, ROWS), 0)
    lane = lax.broadcasted_iota(jnp.int32, (ROWS, ROWS), 1)
    sub_s = lax.broadcasted_iota(jnp.int32, (BUCKETS, ROWS), 0)
    lane_s = lax.broadcasted_iota(jnp.int32, (BUCKETS, ROWS), 1)
    spread = jnp.abs(sub_s - lane_s % BUCKETS)
    table = jnp.zeros((BUCKETS, ROWS), F32)
    for b in range(BUCKETS):
        table = jnp.where(spread == b, ttab[c, b] * (1.0 / SCALE), table)
    part = table.astype(BF16).astype(F32)
    rest = table - part
    middle = rest.astype(BF16).astype(F32)
    table = jnp.where(
        lane_s < 16, part, jnp.where(lane_s < 32, middle, jnp.where(lane_s < 48, rest - middle, 0.0))
    )
    wa[...] = jnp.where(
        (sub >= 48) & (sub < 56) & (lane >= 48) & (lane < 56) & (sub != lane), -FAR, 0.0
    ).astype(BF16)
    wa[pl.ds(0, BUCKETS), :] = table.astype(BF16)

    for w in range(SPAN):
        gap = PAD * ROWS - w * ROWS + sub - lane
        bucket = jnp.minimum(jnp.maximum(gap, 0) // 64, BUCKETS - 1)
        tile = jnp.zeros((ROWS, ROWS), F32)
        low = 2 * (PAD - w) - 2
        for b in range(max(low, 0), min(low + 4, BUCKETS)):
            tile = jnp.where(bucket == b, 0.5 * ptab[c, b], tile)
        if low + 3 >= BUCKETS:
            tile = jnp.where(bucket == BUCKETS - 1, 0.5 * ptab[c, BUCKETS - 1], tile)
        if w == SPAN - 1:
            tile = jnp.where(gap < 0, -4096.0, tile)
        pbias[:, pl.ds(w * ROWS, ROWS)] = tile

    for k in FAR_FIRST:
        m3(k).start()
    own_fv.start()

    for k in range(1, CHIPS):
        m1(k).wait_recv()
        fw(k).start()

    for k in FAR_FIRST:
        m2(k).start()

    ends = [lens[0, 0]]
    for k in range(1, 7):
        ends.append(ends[-1] + lens[0, k])

    def features(block, _):
        t = rb[block, pl.ds(TIM, 16), :].astype(F32)[0:1, :]
        where = block * ROWS + lax.broadcasted_iota(jnp.int32, (1, ROWS), 1)
        user = jnp.zeros((1, ROWS), jnp.int32)
        for end in ends:
            user = user + (where >= end).astype(jnp.int32)
        index = jnp.where(sub < 48, sub % BUCKETS, sub - 48)
        value = jnp.where(sub < 48, t.astype(jnp.int32), jnp.where(sub < 56, user, -1))
        hot = jnp.where(index == value, 1.0, 0.0)
        at = block_rows(block)
        kext[at, pl.ds(ROWS, ROWS)] = jnp.transpose(hot).astype(BF16)
        kext[at, pl.ds(0, ROWS)] = rb[block, pl.ds(KEY, ROWS), :]
        return 0

    lax.fori_loop(0, CHIPS, lambda k, x: features(2 * k + r, x), 0)
    own_fw.wait_recv()
    for k in range(1, CHIPS):
        fw(k).wait_recv()
    lax.fori_loop(0, CHIPS, lambda k, x: features(2 * k + 1 - r, x), 0)

    def att_copy(k):
        t = (c + k) % CHIPS
        return remote(att_s.at[t], att_r.at[c], ats.at[k], atr.at[k], (dp, 2 * t + r))

    def window(b, first, size):
        return pl.ds(pl.multiple_of(b * ROWS + first, ROWS), size)

    def for_reach(t, run):
        for reach in (2, 4, 6, SPAN):
            @pl.when((t == reach // 2 - 1) if reach < SPAN else (t >= 3))
            def _():
                run((SPAN - reach) * ROWS, reach * ROWS)

    def score(k, _):
        t = (c + k) % CHIPS
        b = 2 * t + r
        feat = dot(kext[block_rows(b), pl.ds(ROWS, ROWS)], wa[...]).astype(BF16)
        query = jnp.concatenate([rb[b, pl.ds(QUE, ROWS), :], feat], axis=1)

        def run(start, length):
            for first in range(start, WIN, 256):
                size = min(256, WIN - first)
                x = dot(query, kext[window(b, first, size), :], NT) * (0.5 * SCALE)
                x = x + pbias[:, pl.ds(first, size)]
                th = jnp.tanh(x)
                a = 1.0 + th
                w = x * a
                fsave[t, :, pl.ds(first, size)] = a + w * (1.0 - th)
                wsave[t, :, pl.ds(first, size)] = w.astype(BF16)

        for_reach(t, run)
        return 0

    lax.fori_loop(0, 5, score, 0)
    for k in range(1, CHIPS):
        m3(k).wait_recv()
        fv(k).start()
    lax.fori_loop(5, CHIPS, score, 0)
    own_fv.wait_recv()
    for k in range(1, CHIPS):
        fv(k).wait_recv()

    def attend(k, _):
        t = (c + k) % CHIPS

        def run(start, length):
            total = dot(
                wsave[t, :, pl.ds(start, length)], vall[window(2 * t + r, start, length), :]
            )
            att_s[t] = total.astype(BF16)
            att_t[t] = jnp.transpose(total)

        for_reach(t, run)

        @pl.when(k > 0)
        def _():
            att_copy(k).start()

        tr = att_t[t]
        mean = jnp.sum(tr, axis=0, keepdims=True) * (1.0 / ROWS)
        dev = tr - mean
        row = pl.ds(t, 1)
        stats[c, 0, row, :] = mean
        stats[c, 1, row, :] = jnp.sum(dev * dev, axis=0, keepdims=True)
        return 0

    lax.fori_loop(0, CHIPS, attend, 0)
    for k in range(1, CHIPS):
        m2(k).wait_recv()

    def moments(t, _):
        pn = jnp.transpose(rb[2 * t + r, pl.ds(DNO, ROWS), :].astype(F32))
        pn_t[t] = pn
        g = pn * gcol[...]
        row = pl.ds(t, 1)
        dev = att_t[t] - stats[c, 0, row, :]
        stats[c, 2, row, :] = jnp.sum(dev * g, axis=0, keepdims=True)
        stats[c, 3, row, :] = jnp.sum(g, axis=0, keepdims=True)
        return 0

    lax.fori_loop(0, CHIPS, moments, 0)

    def stat_copy(k):
        to = (c + k) % CHIPS
        return remote(stats.at[c], stats.at[c], sts.at[k], str_.at[k], (dp, 2 * to + r))

    def stat_recv(k):
        source = (c + CHIPS - k) % CHIPS
        return remote(
            stats.at[source], stats.at[source], sts.at[k], str_.at[k], (dp, 2 * source + r)
        )

    for k in FAR_FIRST:
        stat_copy(k).start()
    att_r[c] = att_s[c]
    for k in range(1, 4):
        cy(k).wait_recv()
        cf(k).start()
    for k in range(1, CHIPS):
        stat_recv(k).wait_recv()

    mean = stats[0, 0]
    for h in range(1, HEADS):
        mean = mean + stats[h, 0]
    mean = mean * (1.0 / HEADS)
    spread2 = jnp.zeros((CHIPS, ROWS), F32)
    cross = jnp.zeros((CHIPS, ROWS), F32)
    gsum = jnp.zeros((CHIPS, ROWS), F32)
    for h in range(HEADS):
        off = stats[h, 0] - mean
        spread2 = spread2 + (stats[h, 1] + ROWS * (off * off))
        cross = cross + (stats[h, 2] + off * stats[h, 3])
        gsum = gsum + stats[h, 3]
    inv = lax.rsqrt(spread2 * (1.0 / WIDTH) + EPS)
    comb[0] = mean
    comb[1] = inv
    comb[2] = gsum * (1.0 / WIDTH)
    comb[3] = cross * inv * (1.0 / WIDTH)

    def d_attended(t, _):
        row = pl.ds(t, 1)
        inv_t = comb[1, row, :]
        xhat = (att_t[t] - comb[0, row, :]) * inv_t
        pn = pn_t[t]
        gacc[...] += pn * xhat
        d = inv_t * (pn * gcol[...] - comb[2, row, :] - xhat * comb[3, row, :])
        dout[t] = (0.5 * jnp.transpose(d)).astype(BF16)
        return 0

    lax.fori_loop(0, CHIPS, d_attended, 0)

    def dq_copy(k):
        t = (c + k) % CHIPS
        return remote(mq_s.at[t], mq_r.at[c], qs.at[k], qr.at[k], (dp, 2 * t + r))

    def backward(k, _):
        t = (c + k) % CHIPS
        b = 2 * t + r
        d = dout[t]
        diag[pl.ds(0, ROWS), pl.ds(0, ROWS)] = rb[b, pl.ds(QUE, ROWS), :]
        diag[pl.ds(ROWS, ROWS), pl.ds(ROWS, ROWS)] = d
        both = diag[...]

        def run(start, length):
            at = window(b, start, length)
            some = pl.ds(start, length)
            ds = dot(d, vall[at, :], NT) * fsave[t, :, some]
            pacc[:, some] += ds
            ds = ds.astype(BF16)
            dq_t[...] = dot(ds, kext[at, :])
            dkv[at, :] += dot(jnp.concatenate([ds, wsave[t, :, some]], axis=0), both, TN)

        for_reach(t, run)
        dq = dq_t[...]
        mq_s[t] = (dq[:, :ROWS] * SCALE).astype(BF16)

        @pl.when(k > 0)
        def _():
            dq_copy(k).start()

        high = dq[:, ROWS:].astype(BF16)
        low = (dq[:, ROWS:] - high.astype(F32)).astype(BF16)
        hot = kext[block_rows(b), pl.ds(ROWS, ROWS)]
        tmat[...] += dot(hot, high, TN) + dot(hot, low, TN)
        return 0

    lax.fori_loop(0, 1, backward, 0)

    mine = pl.ds(c, 1)
    mean_c = jnp.transpose(jnp.broadcast_to(comb[0, mine, :], (ROWS, ROWS)))
    inv_c = jnp.transpose(jnp.broadcast_to(comb[1, mine, :], (ROWS, ROWS)))
    for k in range(1, CHIPS):
        att_copy(k).wait_recv()

    def rows_of(h, _):
        normed = (att_r[h].astype(F32) - mean_c) * inv_c * gain[:, columns(h)]
        x = 0.5 * uvqk[:, columns(h)].astype(F32)
        t = jnp.tanh(x)
        a = 1.0 + t
        s = x * a
        hidden = (normed * s.astype(BF16).astype(F32)).astype(BF16)
        hid[:, columns(h)] = hidden
        hid_s[h] = hidden
        d_u = dh[:, columns(h)] * normed
        dpu[:, columns(h)] = (d_u * (0.5 * (a + s * (1.0 - t)))).astype(BF16)
        return 0

    lax.fori_loop(0, HEADS, rows_of, 0)

    def hid_to(j):
        y_to = (y + j // 2) % 4
        r_to = (r + j) % 2
        return remote(
            hid_s.at[2 * y_to + r_to], hid8.at[spot], hs.at[j], hr.at[j],
            (2 * y_to + zl, 2 * c + r_to),
        )

    for j in range(1, 8):
        hid_to(j).start()
    hid8[spot] = hid_s[spot]

    lax.fori_loop(1, CHIPS, backward, 0)

    def to_sibling(t, _):
        at = pl.ds(pl.multiple_of((2 * t + (1 - r) + PAD) * ROWS, ROWS), ROWS)
        xs[t] = dkv[at, :].astype(BF16)
        return 0

    lax.fori_loop(0, CHIPS, to_sibling, 0)
    dkv_copy = remote(xs, xr, sib_s.at[0], sib_r.at[0], (dp, sib))
    dkv_copy.start()

    sums = []
    for b in range(BUCKETS):
        total = jnp.zeros((1, ROWS), F32)
        for w in range(SPAN):
            low = 2 * (PAD - w) - 2
            if low <= b < low + 4 or (b == BUCKETS - 1 and low + 3 >= BUCKETS):
                gap = PAD * ROWS - w * ROWS + sub - lane
                bucket = jnp.minimum(jnp.maximum(gap, 0) // 64, BUCKETS - 1)
                picked = jnp.where(bucket == b, pacc[:, pl.ds(w * ROWS, ROWS)], 0.0)
                total = total + jnp.sum(picked, axis=0, keepdims=True)
        sums.append(total)
    near = tmat[pl.ds(0, BUCKETS), :]
    gap_t = jnp.where(lane_s < BUCKETS, jnp.abs(sub_s - lane_s), -1)
    for b in range(BUCKETS):
        sums.append(jnp.sum(jnp.where(gap_t == b, near, 0.0), axis=0, keepdims=True))
    ones = jnp.ones((8, ROWS), F32)
    sums = jnp.concatenate(sums + [jnp.zeros((ROWS - 2 * BUCKETS, ROWS), F32)], axis=0)
    table_sums = exact_dot(ones, sums, NT)
    gain_sums = exact_dot(ones, gacc[...], NT)
    sub8 = lax.broadcasted_iota(jnp.int32, (8, ROWS), 0)
    tab1[dp] = jnp.where(sub8 == 0, gain_sums, table_sums)

    def t1(k):
        return remote(tab1.at[dp], tab1.at[dp], t1s.at[k], t1r.at[k], ((dp + k) % 8, me))

    def t1_recv(k):
        source = (dp + 8 - k) % 8
        return remote(tab1.at[source], tab1.at[source], t1s.at[k], t1r.at[k], (source, me))

    for k in range(1, 8):
        t1(k).start()

    for j in range(1, 8):
        hid_to(j).wait_recv()
    for k in range(4):
        cf(k).wait_recv()
    left = hid8[...].reshape(8 * ROWS, ROWS)
    for first in range(0, WIDTH // 2, 256):
        parts = [
            dot(left, cot8[:, :, pl.ds(at, 256)].reshape(8 * ROWS, 256), TN).reshape(16, 8, 256)
            for at in (first, first + WIDTH // 2)
        ]
        e_s[:, :, pl.ds(first, 256)] = jnp.concatenate(parts, axis=1).astype(BF16)

    slot = zl * CHIPS + c

    def d2(j):
        to = (me + j) % 16
        return remote(e_s.at[to], e_r.at[slot], d2s.at[j], d2r.at[slot], (2 * y + r, to))

    def d2_recv(j):
        z_from = (zl + j // CHIPS) % 2
        c_from = (c + j % CHIPS) % CHIPS
        here = z_from * CHIPS + c_from
        return remote(
            e_s.at[0], e_r.at[here], d2s.at[0], d2r.at[here], (2 * y + z_from, 2 * c_from + zl)
        )

    for j in range(1, 16):
        d2(j).start()

    @pl.when(r != zl)
    def _():
        d2(0).start()

    @pl.when(r == zl)
    def _():
        e_r[slot] = e_s[me]

    for k in range(1, 8):
        t1_recv(k).wait_recv()
    total = tab1[0]
    for k in range(1, 8):
        total = total + tab1[k]
    tab2[me] = total

    def t2(k):
        return remote(tab2.at[me], tab2.at[me], t2s.at[k], t2r.at[k], (dp, (me + k) % 16))

    def t2_recv(k):
        source = (me + 16 - k) % 16
        return remote(tab2.at[source], tab2.at[source], t2s.at[k], t2r.at[k], (dp, source))

    for k in range(1, 16):
        t2(k).start()

    dkv_copy.wait_recv()

    def kv_copy(k):
        t = (c + k) % CHIPS
        return remote(mk_s.at[t], mk_r.at[c], ks.at[k], kr.at[k], (dp, 2 * t + r))

    def join(k, _):
        t = (c + k) % CHIPS
        at = pl.ds(pl.multiple_of((2 * t + r + PAD) * ROWS, ROWS), ROWS)
        total = dkv[at, :] + xr[t].astype(F32)
        mk_s[t, 0] = (total[:, :ROWS] * SCALE).astype(BF16)
        mk_s[t, 1] = (total[:, ROWS:] * 2.0).astype(BF16)

        @pl.when(k > 0)
        def _():
            kv_copy(k).start()

        return 0

    lax.fori_loop(0, CHIPS, join, 0)
    mq_r[c] = mq_s[c]
    mk_r[c] = mk_s[c]
    load_resid.wait()
    out[...] = (resid[...].astype(F32) + dot(hid[...], wout[...])).astype(BF16)


    for k in range(1, 16):
        t2_recv(k).wait_recv()
    for h in range(HEADS):
        pair = tab2[2 * h] + tab2[2 * h + 1]
        dgain[:, pl.ds(h * ROWS, ROWS)] = pair[0:1]
        dpos[pl.ds(h, 1), :] = pair[1:2, :BUCKETS]
        dtime[pl.ds(h, 1), :] = pair[1:2, BUCKETS : 2 * BUCKETS]

    for j in range(1, 16):
        d2_recv(j).wait_recv()

    @pl.when(r != zl)
    def _():
        d2_recv(0).wait_recv()
        d2(0).wait_send()

    total = e_r[0].astype(F32)
    for k in range(1, 16):
        total = total + e_r[k].astype(F32)
    dwo[:, pl.ds(0, WIDTH // 2)] = total[:8]
    dwo[:, pl.ds(WIDTH // 2, WIDTH // 2)] = total[8:]

    for k in range(1, CHIPS):
        dq_copy(k).wait_recv()
    for k in range(1, CHIPS):
        kv_copy(k).wait_recv()

    own_fw.wait_send()
    own_fv.wait_send()
    dkv_copy.wait_send()
    for k in range(4):
        cf(k).wait_send()
    for k in range(1, CHIPS):
        m1(k).wait_send()
        m2(k).wait_send()
        m3(k).wait_send()
        fw(k).wait_send()
        fv(k).wait_send()
        hid_to(k).wait_send()
        att_copy(k).wait_send()
        stat_copy(k).wait_send()
        dq_copy(k).wait_send()
        kv_copy(k).wait_send()
        t1(k).wait_send()
    for k in range(1, 4):
        cy(k).wait_send()
    for k in range(1, 16):
        d2(k).wait_send()
        t2(k).wait_send()


def finish(uvqk, out_k, dpu, dq, dkv, dwo_k, dgain_k, dpos_k, dtime_k,
           out, dpre, dwo, dgain, dpos, dtime):
    out[...] = out_k[...]
    dpre[:, pl.ds(0, WIDTH)] = dpu[...]
    for h in range(HEADS):
        for group, value in ((1, dkv[h, 1]), (2, dq[h]), (3, dkv[h, 0])):
            at = pl.ds((group * HEADS + h) * ROWS, ROWS)
            x = 0.5 * uvqk[:, at].astype(F32)
            dpre[:, at] = (value.astype(F32) * silu_grad_half(x)).astype(BF16)
    dwo[...] = dwo_k[...]
    dgain[...] = dgain_k[...]
    dpos[...] = dpos_k[...]
    dtime[...] = dtime_k[...]


def body(
    uvqk, residual, lengths, time_buckets, pos_table, time_table, output_norm_gain, w_out, cotangent
):
    vm = pl.BlockSpec(memory_space=pltpu.VMEM)
    sm = pl.BlockSpec(memory_space=pltpu.SMEM)
    hbm = pl.BlockSpec(memory_space=pl.ANY)
    tile = (ROWS, ROWS)
    dma = pltpu.SemaphoreType.DMA
    padded = (2 * CHIPS + PAD) * ROWS
    scratch = [
        pltpu.VMEM((ROWS, 4 * WIDTH), BF16),
        pltpu.VMEM((ROWS, WIDTH), BF16),
        pltpu.VMEM((WIDTH, WIDTH), BF16),
        pltpu.VMEM((8, ROWS, WIDTH), BF16),
        pltpu.VMEM((HEADS, END, ROWS), BF16),
        pltpu.VMEM((2 * CHIPS, END, ROWS), BF16),
        pltpu.VMEM((ROWS, WIDTH), F32),
        pltpu.VMEM((padded, 2 * ROWS), BF16),
        pltpu.VMEM((padded, ROWS), BF16),
        pltpu.VMEM(tile, BF16),
        pltpu.VMEM((ROWS, WIN), F32),
        pltpu.VMEM((CHIPS, ROWS, WIN), BF16),
        pltpu.VMEM((CHIPS, ROWS, WIN), F32),
        pltpu.VMEM((CHIPS,) + tile, F32),
        pltpu.VMEM((CHIPS,) + tile, F32),
        pltpu.VMEM(tile, F32),
        pltpu.VMEM((CHIPS,) + tile, BF16),
        pltpu.VMEM((HEADS,) + tile, BF16),
        pltpu.VMEM((HEADS, 4, CHIPS, ROWS), F32),
        pltpu.VMEM((4, CHIPS, ROWS), F32),
        pltpu.VMEM((CHIPS,) + tile, BF16),
        pltpu.VMEM((ROWS, WIDTH), BF16),
        pltpu.VMEM((8,) + tile, BF16),
        pltpu.VMEM((8,) + tile, BF16),
        pltpu.VMEM((16, 16, WIDTH // 2), BF16),
        pltpu.VMEM((16, 16, WIDTH // 2), BF16),
        pltpu.VMEM((2 * ROWS, 2 * ROWS), BF16),
        pltpu.VMEM((ROWS, 2 * ROWS), F32),
        pltpu.VMEM((padded, 2 * ROWS), F32),
        pltpu.VMEM((ROWS, WIN), F32),
        pltpu.VMEM(tile, F32),
        pltpu.VMEM(tile, F32),
        pltpu.VMEM((CHIPS,) + tile, BF16),
        pltpu.VMEM((CHIPS, ROWS, 2 * ROWS), BF16),
        pltpu.VMEM((CHIPS, ROWS, 2 * ROWS), BF16),
        pltpu.VMEM((CHIPS, 2) + tile, BF16),
        pltpu.VMEM((8, 8, ROWS), F32),
        pltpu.VMEM((16, 8, ROWS), F32),
        dma((4,)),
    ] + [
        dma((count,))
        for count in (
            8, 8, 8, 8, 8, 8, 8, 8, 8, 8, 1, 1, 8, 8, 8, 8,
            4, 4, 4, 4, 8, 8, 16, 16, 8, 8, 8, 8, 8, 8, 16, 16,
        )
    ]
    partial = pl.pallas_call(
        kernel,
        out_shape=(
            jax.ShapeDtypeStruct((ROWS, WIDTH), BF16),
            jax.ShapeDtypeStruct((ROWS, WIDTH), BF16),
            jax.ShapeDtypeStruct((HEADS,) + tile, BF16),
            jax.ShapeDtypeStruct((HEADS, 2) + tile, BF16),
            jax.ShapeDtypeStruct((8, WIDTH), F32),
            jax.ShapeDtypeStruct((1, WIDTH), F32),
            jax.ShapeDtypeStruct((HEADS, BUCKETS), F32),
            jax.ShapeDtypeStruct((HEADS, BUCKETS), F32),
        ),
        in_specs=[hbm, hbm, sm, vm, sm, sm, vm, hbm, hbm],
        out_specs=(vm,) * 8,
        scratch_shapes=scratch,
        compiler_params=pltpu.CompilerParams(
            collective_id=0, has_side_effects=True, vmem_limit_bytes=63 * 1024 * 1024
        ),
    )(
        uvqk[0], residual[0], lengths, time_buckets, pos_table, time_table,
        output_norm_gain[None], w_out, cotangent[0],
    )
    steps = 2
    some = ROWS // steps

    def whole(*shape):
        return pl.BlockSpec(shape, lambda i: (0,) * len(shape))

    wide = pl.BlockSpec((some, 4 * WIDTH), lambda i: (i, 0))
    narrow = pl.BlockSpec((some, WIDTH), lambda i: (i, 0))
    small = [whole(8, WIDTH), whole(1, WIDTH), whole(HEADS, BUCKETS), whole(HEADS, BUCKETS)]
    out, dpre, dwo, dgain, dpos, dtime = pl.pallas_call(
        finish,
        grid=(steps,),
        out_shape=(
            jax.ShapeDtypeStruct((ROWS, WIDTH), BF16),
            jax.ShapeDtypeStruct((ROWS, 4 * WIDTH), BF16),
            jax.ShapeDtypeStruct((8, WIDTH), F32),
            jax.ShapeDtypeStruct((1, WIDTH), F32),
            jax.ShapeDtypeStruct((HEADS, BUCKETS), F32),
            jax.ShapeDtypeStruct((HEADS, BUCKETS), F32),
        ),
        in_specs=[
            wide, narrow, narrow,
            pl.BlockSpec((HEADS, some, ROWS), lambda i: (0, i, 0)),
            pl.BlockSpec((HEADS, 2, some, ROWS), lambda i: (0, 0, i, 0)),
        ] + small,
        out_specs=[narrow, wide] + small,
        compiler_params=pltpu.CompilerParams(vmem_limit_bytes=63 * 1024 * 1024),
    )(uvqk[0], *partial)
    return (out[None], dpre[None], dwo, dgain[0], dpos, dtime)


def solution(mesh):
    in_specs = (
        P("dp", "ctx", None),
        P("dp", "ctx", None),
        P("dp", None),
        P("dp", "ctx"),
        P(),
        P(),
        P(),
        P(),
        P("dp", "ctx", None),
    )
    out_specs = (P("dp", "ctx", None), P("dp", "ctx", None), P(("dp", "ctx"), None), P(), P(), P())
    return jax.shard_map(body, mesh=mesh, in_specs=in_specs, out_specs=out_specs, check_vma=False)
```

```python
import jax
import jax.numpy as jnp
from jax import lax
from jax.experimental import pallas as pl
from jax.experimental.pallas import tpu as pltpu
from jax.sharding import PartitionSpec as P

MESH = pl.DeviceIdType.MESH
F32 = jnp.float32
BF16 = jnp.bfloat16

HEADS = 8
EPS = 1e-05
ROWS = 128
CHIPS = 8
SPAN = 9
WIN = SPAN * ROWS
PAD = SPAN - 1
FAR_FIRST = (5, 3, 4, 7, 1, 2, 6)
WIDTH = HEADS * ROWS
BUCKETS = 16
FAR = 131072.0
SCALE = ROWS ** (-0.5)

KEY, TIM, QUE, VAL, DNO, END = 0, 128, 144, 272, 400, 528
CHUNKS = [(0, 256), (256, 256), (512, 256), (768, 256), (1024, 128)]

NT = (((1,), (1,)), ((), ()))
TN = (((0,), (0,)), ((), ()))
NN = (((1,), (0,)), ((), ()))


def dot(a, b, dims=NN):
    return lax.dot_general(a, b, dims, preferred_element_type=F32)


def exact_dot(a, b, dims=NN):
    return lax.dot_general(
        a, b, dims, preferred_element_type=F32, precision=lax.Precision.HIGHEST
    )


def silu_half(x):
    return x * (1.0 + jnp.tanh(x))


def silu_grad_half(x):
    t = jnp.tanh(x)
    a = 1.0 + t
    return 0.5 * (a + x * a * (1.0 - t))


def columns(h):
    return pl.ds(pl.multiple_of(h * ROWS, ROWS), ROWS)


def kernel(
    uvqk_h, resid_h, lens, times, ptab, ttab, gain, wout_h, cot_h,
    out_h, dpu_h, mq_r, mk_r, dwo, dgain, dpos, dtime,
    out, dpu, uvqk, resid, wout, cot8, sb, rb, dh, kext, vall, wa, pbias, wsave, fsave,
    att_t, pn_t, gcol, att_s, att_r, stats, comb, dout, hid, hid_s, hid8,
    e_s, e_r, diag, dq_t, dkv, pacc, tmat, gacc, mq_s, xs, xr, mk_s, tab1, tab2,
    loc_sem, m1s, m1r, m2s, m2r, m3s, m3r, fws, fwr, fvs, fvr, sib_s, sib_r, ats, atr, sts, str_,
    cys, cyr, cfs, cfr, hs, hr, d2s, d2r, qs, qr, ks, kr, t1s, t1r, t2s, t2r,
):
    dp = lax.axis_index("dp")
    me = lax.axis_index("ctx")
    c = me // 2
    r = me % 2
    y = dp // 2
    zl = dp % 2
    sib = 2 * c + (1 - r)
    spot = 2 * y + r

    def remote(src, dst, ssem, rsem, to):
        return pltpu.make_async_remote_copy(
            src_ref=src, dst_ref=dst, send_sem=ssem, recv_sem=rsem, device_id=to,
            device_id_type=MESH,
        )

    load_uvqk = pltpu.make_async_copy(uvqk_h, uvqk, loc_sem.at[0])
    load_cot = pltpu.make_async_copy(cot_h, cot8.at[spot], loc_sem.at[1])
    load_wout = pltpu.make_async_copy(wout_h, wout, loc_sem.at[2])
    load_resid = pltpu.make_async_copy(resid_h, resid, loc_sem.at[3])
    load_uvqk.start()
    load_cot.start()
    load_wout.start()
    load_resid.start()

    barrier = pltpu.get_barrier_semaphore()

    def greet(j, _):
        pl.semaphore_signal(
            barrier, inc=1, device_id=(2 * y + (zl + j // 16) % 2, (me + j % 16) % 16),
            device_id_type=MESH,
        )
        return 0

    lax.fori_loop(1, 32, greet, 0)

    def greet_far(j, _):
        pl.semaphore_signal(
            barrier, inc=1, device_id=(2 * ((y + 1 + j // 2) % 4) + j % 2, me),
            device_id_type=MESH,
        )
        return 0

    lax.fori_loop(0, 6, greet_far, 0)

    time_rows = jnp.broadcast_to(times[...].astype(F32), (16, ROWS)).astype(BF16)

    def activate(h, _):
        for group, where in ((3, KEY), (2, QUE)):
            x = 0.5 * uvqk[:, columns(group * HEADS + h)].astype(F32)
            sb[h, pl.ds(where, ROWS), :] = silu_half(x).astype(BF16)
        sb[h, pl.ds(TIM, 16), :] = time_rows
        return 0

    load_uvqk.wait()
    lax.fori_loop(0, HEADS, activate, 0)
    pl.semaphore_wait(barrier, 37)

    def block_rows(block):
        return pl.ds(pl.multiple_of((block + PAD) * ROWS, ROWS), ROWS)

    def m1(k):
        to = (c + k) % CHIPS
        return remote(
            sb.at[to, pl.ds(0, VAL)], rb.at[me, pl.ds(0, VAL)], m1s.at[k], m1r.at[k],
            (dp, 2 * to + r),
        )

    def m2(k):
        to = (c + k) % CHIPS
        return remote(
            sb.at[to, pl.ds(DNO, ROWS)], rb.at[me, pl.ds(DNO, ROWS)], m2s.at[k], m2r.at[k],
            (dp, 2 * to + r),
        )

    def m3(k):
        to = (c + k) % CHIPS
        return remote(
            sb.at[to, pl.ds(VAL, ROWS)], vall.at[block_rows(me)], m3s.at[k], m3r.at[k],
            (dp, 2 * to + r),
        )

    own_fw = remote(
        sb.at[c, pl.ds(0, QUE)], rb.at[me, pl.ds(0, QUE)], fws.at[0], fwr.at[0], (dp, sib)
    )
    own_fv = remote(
        sb.at[c, pl.ds(VAL, ROWS)], vall.at[block_rows(me)], fvs.at[0], fvr.at[0], (dp, sib)
    )

    def fw(k):
        block = 2 * ((c + CHIPS - k) % CHIPS) + r
        return remote(
            rb.at[block, pl.ds(0, QUE)], rb.at[block, pl.ds(0, QUE)], fws.at[k], fwr.at[k],
            (dp, sib),
        )

    def fv(k):
        at = block_rows(2 * ((c + CHIPS - k) % CHIPS) + r)
        return remote(vall.at[at], vall.at[at], fvs.at[k], fvr.at[k], (dp, sib))

    def cy(k):
        return remote(
            cot8.at[spot], cot8.at[spot], cys.at[k], cyr.at[k], (2 * ((y + k) % 4) + zl, me)
        )

    def cf(k):
        at = 2 * ((y + 4 - k) % 4) + r
        return remote(cot8.at[at], cot8.at[at], cfs.at[k], cfr.at[k], (dp, sib))

    for k in FAR_FIRST:
        m1(k).start()
    own_fw.start()

    def activate_values(h, _):
        x = 0.5 * uvqk[:, columns(HEADS + h)].astype(F32)
        sb[h, pl.ds(VAL, ROWS), :] = silu_half(x).astype(BF16)
        return 0

    lax.fori_loop(0, HEADS, activate_values, 0)
    rb[me, pl.ds(0, VAL), :] = sb[c, pl.ds(0, VAL), :]
    vall[block_rows(me), :] = sb[c, pl.ds(VAL, ROWS), :]
    load_cot.wait()
    for k in range(1, 4):
        cy(k).start()
    cf(0).start()

    load_wout.wait()
    dh[...] = dot(cot8[spot], wout[...], NT)

    def d_normed(h, _):
        x = 0.5 * uvqk[:, columns(h)].astype(F32)
        u = silu_half(x).astype(BF16).astype(F32)
        sb[h, pl.ds(DNO, ROWS), :] = (dh[:, columns(h)] * u).astype(BF16)
        return 0

    lax.fori_loop(0, HEADS, d_normed, 0)
    rb[me, pl.ds(DNO, ROWS), :] = sb[c, pl.ds(DNO, ROWS), :]

    kext[pl.ds(0, PAD * ROWS), :] = jnp.zeros((PAD * ROWS, 2 * ROWS), BF16)
    vall[pl.ds(0, PAD * ROWS), :] = jnp.zeros((PAD * ROWS, ROWS), BF16)
    dkv[...] = jnp.zeros_like(dkv)
    pacc[...] = jnp.zeros_like(pacc)
    tmat[...] = jnp.zeros_like(tmat)
    gacc[...] = jnp.zeros_like(gacc)
    diag[...] = jnp.zeros_like(diag)
    gcol[...] = jnp.transpose(jnp.broadcast_to(gain[:, columns(c)], (ROWS, ROWS)))

    sub = lax.broadcasted_iota(jnp.int32, (ROWS, ROWS), 0)
    lane = lax.broadcasted_iota(jnp.int32, (ROWS, ROWS), 1)
    sub_s = lax.broadcasted_iota(jnp.int32, (BUCKETS, ROWS), 0)
    lane_s = lax.broadcasted_iota(jnp.int32, (BUCKETS, ROWS), 1)
    spread = jnp.abs(sub_s - lane_s % BUCKETS)
    table = jnp.zeros((BUCKETS, ROWS), F32)
    for b in range(BUCKETS):
        table = jnp.where(spread == b, ttab[c, b] * (1.0 / SCALE), table)
    part = table.astype(BF16).astype(F32)
    rest = table - part
    middle = rest.astype(BF16).astype(F32)
    table = jnp.where(
        lane_s < 16, part, jnp.where(lane_s < 32, middle, jnp.where(lane_s < 48, rest - middle, 0.0))
    )
    wa[...] = jnp.where(
        (sub >= 48) & (sub < 56) & (lane >= 48) & (lane < 56) & (sub != lane), -FAR, 0.0
    ).astype(BF16)
    wa[pl.ds(0, BUCKETS), :] = table.astype(BF16)

    for w in range(SPAN):
        gap = PAD * ROWS - w * ROWS + sub - lane
        bucket = jnp.minimum(jnp.maximum(gap, 0) // 64, BUCKETS - 1)
        tile = jnp.zeros((ROWS, ROWS), F32)
        low = 2 * (PAD - w) - 2
        for b in range(max(low, 0), min(low + 4, BUCKETS)):
            tile = jnp.where(bucket == b, 0.5 * ptab[c, b], tile)
        if low + 3 >= BUCKETS:
            tile = jnp.where(bucket == BUCKETS - 1, 0.5 * ptab[c, BUCKETS - 1], tile)
        if w == SPAN - 1:
            tile = jnp.where(gap < 0, -4096.0, tile)
        pbias[:, pl.ds(w * ROWS, ROWS)] = tile

    for k in FAR_FIRST:
        m3(k).start()
    own_fv.start()

    for k in range(1, CHIPS):
        m1(k).wait_recv()
        fw(k).start()

    for k in FAR_FIRST:
        m2(k).start()

    ends = [lens[0, 0]]
    for k in range(1, 7):
        ends.append(ends[-1] + lens[0, k])

    def features(block, _):
        t = rb[block, pl.ds(TIM, 16), :].astype(F32)[0:1, :]
        where = block * ROWS + lax.broadcasted_iota(jnp.int32, (1, ROWS), 1)
        user = jnp.zeros((1, ROWS), jnp.int32)
        for end in ends:
            user = user + (where >= end).astype(jnp.int32)
        index = jnp.where(sub < 48, sub % BUCKETS, sub - 48)
        value = jnp.where(sub < 48, t.astype(jnp.int32), jnp.where(sub < 56, user, -1))
        hot = jnp.where(index == value, 1.0, 0.0)
        at = block_rows(block)
        kext[at, pl.ds(ROWS, ROWS)] = jnp.transpose(hot).astype(BF16)
        kext[at, pl.ds(0, ROWS)] = rb[block, pl.ds(KEY, ROWS), :]
        return 0

    lax.fori_loop(0, CHIPS, lambda k, x: features(2 * k + r, x), 0)
    own_fw.wait_recv()
    for k in range(1, CHIPS):
        fw(k).wait_recv()
    lax.fori_loop(0, CHIPS, lambda k, x: features(2 * k + 1 - r, x), 0)

    def att_copy(k):
        t = (c + k) % CHIPS
        return remote(att_s.at[t], att_r.at[c], ats.at[k], atr.at[k], (dp, 2 * t + r))

    def window(b, first, size):
        return pl.ds(pl.multiple_of(b * ROWS + first, ROWS), size)

    def for_reach(t, run):
        for reach in (2, 4, 6, SPAN):
            @pl.when((t == reach // 2 - 1) if reach < SPAN else (t >= 3))
            def _():
                run((SPAN - reach) * ROWS, reach * ROWS)

    def score(k, _):
        t = (c + k) % CHIPS
        b = 2 * t + r
        feat = dot(kext[block_rows(b), pl.ds(ROWS, ROWS)], wa[...]).astype(BF16)
        query = jnp.concatenate([rb[b, pl.ds(QUE, ROWS), :], feat], axis=1)

        def run(start, length):
            for first in range(start, WIN, 256):
                size = min(256, WIN - first)
                x = dot(query, kext[window(b, first, size), :], NT) * (0.5 * SCALE)
                x = x + pbias[:, pl.ds(first, size)]
                th = jnp.tanh(x)
                a = 1.0 + th
                w = x * a
                fsave[t, :, pl.ds(first, size)] = a + w * (1.0 - th)
                wsave[t, :, pl.ds(first, size)] = w.astype(BF16)

        for_reach(t, run)
        return 0

    lax.fori_loop(0, 5, score, 0)
    for k in range(1, CHIPS):
        m3(k).wait_recv()
        fv(k).start()
    lax.fori_loop(5, CHIPS, score, 0)
    own_fv.wait_recv()
    for k in range(1, CHIPS):
        fv(k).wait_recv()

    def attend(k, _):
        t = (c + k) % CHIPS

        def run(start, length):
            total = dot(
                wsave[t, :, pl.ds(start, length)], vall[window(2 * t + r, start, length), :]
            )
            att_s[t] = total.astype(BF16)
            att_t[t] = jnp.transpose(total)

        for_reach(t, run)

        @pl.when(k > 0)
        def _():
            att_copy(k).start()

        tr = att_t[t]
        mean = jnp.sum(tr, axis=0, keepdims=True) * (1.0 / ROWS)
        dev = tr - mean
        row = pl.ds(t, 1)
        stats[c, 0, row, :] = mean
        stats[c, 1, row, :] = jnp.sum(dev * dev, axis=0, keepdims=True)
        return 0

    lax.fori_loop(0, CHIPS, attend, 0)
    for k in range(1, CHIPS):
        m2(k).wait_recv()

    def moments(t, _):
        pn = jnp.transpose(rb[2 * t + r, pl.ds(DNO, ROWS), :].astype(F32))
        pn_t[t] = pn
        g = pn * gcol[...]
        row = pl.ds(t, 1)
        dev = att_t[t] - stats[c, 0, row, :]
        stats[c, 2, row, :] = jnp.sum(dev * g, axis=0, keepdims=True)
        stats[c, 3, row, :] = jnp.sum(g, axis=0, keepdims=True)
        return 0

    lax.fori_loop(0, CHIPS, moments, 0)

    def stat_copy(k):
        to = (c + k) % CHIPS
        return remote(stats.at[c], stats.at[c], sts.at[k], str_.at[k], (dp, 2 * to + r))

    def stat_recv(k):
        source = (c + CHIPS - k) % CHIPS
        return remote(
            stats.at[source], stats.at[source], sts.at[k], str_.at[k], (dp, 2 * source + r)
        )

    for k in FAR_FIRST:
        stat_copy(k).start()
    att_r[c] = att_s[c]
    for k in range(1, 4):
        cy(k).wait_recv()
        cf(k).start()
    for k in range(1, CHIPS):
        stat_recv(k).wait_recv()

    mean = stats[0, 0]
    for h in range(1, HEADS):
        mean = mean + stats[h, 0]
    mean = mean * (1.0 / HEADS)
    spread2 = jnp.zeros((CHIPS, ROWS), F32)
    cross = jnp.zeros((CHIPS, ROWS), F32)
    gsum = jnp.zeros((CHIPS, ROWS), F32)
    for h in range(HEADS):
        off = stats[h, 0] - mean
        spread2 = spread2 + (stats[h, 1] + ROWS * (off * off))
        cross = cross + (stats[h, 2] + off * stats[h, 3])
        gsum = gsum + stats[h, 3]
    inv = lax.rsqrt(spread2 * (1.0 / WIDTH) + EPS)
    comb[0] = mean
    comb[1] = inv
    comb[2] = gsum * (1.0 / WIDTH)
    comb[3] = cross * inv * (1.0 / WIDTH)

    def d_attended(t, _):
        row = pl.ds(t, 1)
        inv_t = comb[1, row, :]
        xhat = (att_t[t] - comb[0, row, :]) * inv_t
        pn = pn_t[t]
        gacc[...] += pn * xhat
        d = inv_t * (pn * gcol[...] - comb[2, row, :] - xhat * comb[3, row, :])
        dout[t] = (0.5 * jnp.transpose(d)).astype(BF16)
        return 0

    lax.fori_loop(0, CHIPS, d_attended, 0)

    def dq_copy(k):
        t = (c + k) % CHIPS
        return remote(mq_s.at[t], mq_r.at[c], qs.at[k], qr.at[k], (dp, 2 * t + r))

    def backward(k, _):
        t = (c + k) % CHIPS
        b = 2 * t + r
        d = dout[t]
        diag[pl.ds(0, ROWS), pl.ds(0, ROWS)] = rb[b, pl.ds(QUE, ROWS), :]
        diag[pl.ds(ROWS, ROWS), pl.ds(ROWS, ROWS)] = d
        both = diag[...]

        def run(start, length):
            at = window(b, start, length)
            some = pl.ds(start, length)
            ds = dot(d, vall[at, :], NT) * fsave[t, :, some]
            pacc[:, some] += ds
            ds = ds.astype(BF16)
            dq_t[...] = dot(ds, kext[at, :])
            dkv[at, :] += dot(jnp.concatenate([ds, wsave[t, :, some]], axis=0), both, TN)

        for_reach(t, run)
        dq = dq_t[...]
        mq_s[t] = (dq[:, :ROWS] * SCALE).astype(BF16)

        @pl.when(k > 0)
        def _():
            dq_copy(k).start()

        high = dq[:, ROWS:].astype(BF16)
        low = (dq[:, ROWS:] - high.astype(F32)).astype(BF16)
        hot = kext[block_rows(b), pl.ds(ROWS, ROWS)]
        tmat[...] += dot(hot, high, TN) + dot(hot, low, TN)
        return 0

    lax.fori_loop(0, 1, backward, 0)

    mine = pl.ds(c, 1)
    mean_c = jnp.transpose(jnp.broadcast_to(comb[0, mine, :], (ROWS, ROWS)))
    inv_c = jnp.transpose(jnp.broadcast_to(comb[1, mine, :], (ROWS, ROWS)))
    for k in range(1, CHIPS):
        att_copy(k).wait_recv()

    def rows_of(h, _):
        normed = (att_r[h].astype(F32) - mean_c) * inv_c * gain[:, columns(h)]
        x = 0.5 * uvqk[:, columns(h)].astype(F32)
        t = jnp.tanh(x)
        a = 1.0 + t
        s = x * a
        hidden = (normed * s.astype(BF16).astype(F32)).astype(BF16)
        hid[:, columns(h)] = hidden
        hid_s[h] = hidden
        d_u = dh[:, columns(h)] * normed
        dpu[:, columns(h)] = (d_u * (0.5 * (a + s * (1.0 - t)))).astype(BF16)
        return 0

    lax.fori_loop(0, HEADS, rows_of, 0)
    store_dpu = pltpu.make_async_copy(dpu, dpu_h, loc_sem.at[7])
    store_dpu.start()

    def hid_to(j):
        y_to = (y + j // 2) % 4
        r_to = (r + j) % 2
        return remote(
            hid_s.at[2 * y_to + r_to], hid8.at[spot], hs.at[j], hr.at[j],
            (2 * y_to + zl, 2 * c + r_to),
        )

    for j in range(1, 8):
        hid_to(j).start()
    hid8[spot] = hid_s[spot]

    lax.fori_loop(1, CHIPS, backward, 0)

    def to_sibling(t, _):
        at = pl.ds(pl.multiple_of((2 * t + (1 - r) + PAD) * ROWS, ROWS), ROWS)
        xs[t] = dkv[at, :].astype(BF16)
        return 0

    lax.fori_loop(0, CHIPS, to_sibling, 0)
    dkv_copy = remote(xs, xr, sib_s.at[0], sib_r.at[0], (dp, sib))
    dkv_copy.start()

    sums = []
    for b in range(BUCKETS):
        total = jnp.zeros((1, ROWS), F32)
        for w in range(SPAN):
            low = 2 * (PAD - w) - 2
            if low <= b < low + 4 or (b == BUCKETS - 1 and low + 3 >= BUCKETS):
                gap = PAD * ROWS - w * ROWS + sub - lane
                bucket = jnp.minimum(jnp.maximum(gap, 0) // 64, BUCKETS - 1)
                picked = jnp.where(bucket == b, pacc[:, pl.ds(w * ROWS, ROWS)], 0.0)
                total = total + jnp.sum(picked, axis=0, keepdims=True)
        sums.append(total)
    near = tmat[pl.ds(0, BUCKETS), :]
    gap_t = jnp.where(lane_s < BUCKETS, jnp.abs(sub_s - lane_s), -1)
    for b in range(BUCKETS):
        sums.append(jnp.sum(jnp.where(gap_t == b, near, 0.0), axis=0, keepdims=True))
    ones = jnp.ones((8, ROWS), F32)
    sums = jnp.concatenate(sums + [jnp.zeros((ROWS - 2 * BUCKETS, ROWS), F32)], axis=0)
    table_sums = exact_dot(ones, sums, NT)
    gain_sums = exact_dot(ones, gacc[...], NT)
    sub8 = lax.broadcasted_iota(jnp.int32, (8, ROWS), 0)
    tab1[dp] = jnp.where(sub8 == 0, gain_sums, table_sums)

    def t1(k):
        return remote(tab1.at[dp], tab1.at[dp], t1s.at[k], t1r.at[k], ((dp + k) % 8, me))

    def t1_recv(k):
        source = (dp + 8 - k) % 8
        return remote(tab1.at[source], tab1.at[source], t1s.at[k], t1r.at[k], (source, me))

    for k in range(1, 8):
        t1(k).start()

    for j in range(1, 8):
        hid_to(j).wait_recv()
    for k in range(4):
        cf(k).wait_recv()
    left = hid8[...].reshape(8 * ROWS, ROWS)
    for first in range(0, WIDTH // 2, 256):
        parts = [
            dot(left, cot8[:, :, pl.ds(at, 256)].reshape(8 * ROWS, 256), TN).reshape(16, 8, 256)
            for at in (first, first + WIDTH // 2)
        ]
        e_s[:, :, pl.ds(first, 256)] = jnp.concatenate(parts, axis=1).astype(BF16)

    slot = zl * CHIPS + c

    def d2(j):
        to = (me + j) % 16
        return remote(e_s.at[to], e_r.at[slot], d2s.at[j], d2r.at[slot], (2 * y + r, to))

    def d2_recv(j):
        z_from = (zl + j // CHIPS) % 2
        c_from = (c + j % CHIPS) % CHIPS
        here = z_from * CHIPS + c_from
        return remote(
            e_s.at[0], e_r.at[here], d2s.at[0], d2r.at[here], (2 * y + z_from, 2 * c_from + zl)
        )

    for j in range(1, 16):
        d2(j).start()

    @pl.when(r != zl)
    def _():
        d2(0).start()

    @pl.when(r == zl)
    def _():
        e_r[slot] = e_s[me]

    for k in range(1, 8):
        t1_recv(k).wait_recv()
    total = tab1[0]
    for k in range(1, 8):
        total = total + tab1[k]
    tab2[me] = total

    def t2(k):
        return remote(tab2.at[me], tab2.at[me], t2s.at[k], t2r.at[k], (dp, (me + k) % 16))

    def t2_recv(k):
        source = (me + 16 - k) % 16
        return remote(tab2.at[source], tab2.at[source], t2s.at[k], t2r.at[k], (dp, source))

    for k in range(1, 16):
        t2(k).start()

    dkv_copy.wait_recv()

    def kv_copy(k):
        t = (c + k) % CHIPS
        return remote(mk_s.at[t], mk_r.at[c], ks.at[k], kr.at[k], (dp, 2 * t + r))

    def join(k, _):
        t = (c + k) % CHIPS
        at = pl.ds(pl.multiple_of((2 * t + r + PAD) * ROWS, ROWS), ROWS)
        total = dkv[at, :] + xr[t].astype(F32)
        mk_s[t, 0] = (total[:, :ROWS] * SCALE).astype(BF16)
        mk_s[t, 1] = (total[:, ROWS:] * 2.0).astype(BF16)

        @pl.when(k > 0)
        def _():
            kv_copy(k).start()

        return 0

    lax.fori_loop(0, CHIPS, join, 0)
    own_dq = pltpu.make_async_copy(mq_s.at[c], mq_r.at[c], loc_sem.at[4])
    own_kv = pltpu.make_async_copy(mk_s.at[c], mk_r.at[c], loc_sem.at[5])
    own_dq.start()
    own_kv.start()
    load_resid.wait()
    out[...] = (resid[...].astype(F32) + dot(hid[...], wout[...])).astype(BF16)
    store_out = pltpu.make_async_copy(out, out_h, loc_sem.at[6])
    store_out.start()


    for k in range(1, 16):
        t2_recv(k).wait_recv()
    for h in range(HEADS):
        pair = tab2[2 * h] + tab2[2 * h + 1]
        dgain[:, pl.ds(h * ROWS, ROWS)] = pair[0:1]
        dpos[pl.ds(h, 1), :] = pair[1:2, :BUCKETS]
        dtime[pl.ds(h, 1), :] = pair[1:2, BUCKETS : 2 * BUCKETS]

    for j in range(1, 16):
        d2_recv(j).wait_recv()

    @pl.when(r != zl)
    def _():
        d2_recv(0).wait_recv()
        d2(0).wait_send()

    total = e_r[0].astype(F32)
    for k in range(1, 16):
        total = total + e_r[k].astype(F32)
    dwo[:, pl.ds(0, WIDTH // 2)] = total[:8]
    dwo[:, pl.ds(WIDTH // 2, WIDTH // 2)] = total[8:]

    for k in range(1, CHIPS):
        dq_copy(k).wait_recv()
    for k in range(1, CHIPS):
        kv_copy(k).wait_recv()

    own_dq.wait()
    own_kv.wait()
    store_out.wait()
    store_dpu.wait()
    own_fw.wait_send()
    own_fv.wait_send()
    dkv_copy.wait_send()
    for k in range(4):
        cf(k).wait_send()
    for k in range(1, CHIPS):
        m1(k).wait_send()
        m2(k).wait_send()
        m3(k).wait_send()
        fw(k).wait_send()
        fv(k).wait_send()
        hid_to(k).wait_send()
        att_copy(k).wait_send()
        stat_copy(k).wait_send()
        dq_copy(k).wait_send()
        kv_copy(k).wait_send()
        t1(k).wait_send()
    for k in range(1, 4):
        cy(k).wait_send()
    for k in range(1, 16):
        d2(k).wait_send()
        t2(k).wait_send()


def finish(uvqk, out_k, dpu, dq, dkv, dwo_k, dgain_k, dpos_k, dtime_k,
           out, dpre, dwo, dgain, dpos, dtime):
    out[...] = out_k[...]
    dpre[:, pl.ds(0, WIDTH)] = dpu[...]
    for h in range(HEADS):
        for group, value in ((1, dkv[h, 1]), (2, dq[h]), (3, dkv[h, 0])):
            at = pl.ds((group * HEADS + h) * ROWS, ROWS)
            x = 0.5 * uvqk[:, at].astype(F32)
            dpre[:, at] = (value.astype(F32) * silu_grad_half(x)).astype(BF16)
    dwo[...] = dwo_k[...]
    dgain[...] = dgain_k[...]
    dpos[...] = dpos_k[...]
    dtime[...] = dtime_k[...]


def body(
    uvqk, residual, lengths, time_buckets, pos_table, time_table, output_norm_gain, w_out, cotangent
):
    vm = pl.BlockSpec(memory_space=pltpu.VMEM)
    sm = pl.BlockSpec(memory_space=pltpu.SMEM)
    hbm = pl.BlockSpec(memory_space=pl.ANY)
    tile = (ROWS, ROWS)
    dma = pltpu.SemaphoreType.DMA
    padded = (2 * CHIPS + PAD) * ROWS
    scratch = [
        pltpu.VMEM((ROWS, WIDTH), BF16),
        pltpu.VMEM((ROWS, WIDTH), BF16),
        pltpu.VMEM((ROWS, 4 * WIDTH), BF16),
        pltpu.VMEM((ROWS, WIDTH), BF16),
        pltpu.VMEM((WIDTH, WIDTH), BF16),
        pltpu.VMEM((8, ROWS, WIDTH), BF16),
        pltpu.VMEM((HEADS, END, ROWS), BF16),
        pltpu.VMEM((2 * CHIPS, END, ROWS), BF16),
        pltpu.VMEM((ROWS, WIDTH), F32),
        pltpu.VMEM((padded, 2 * ROWS), BF16),
        pltpu.VMEM((padded, ROWS), BF16),
        pltpu.VMEM(tile, BF16),
        pltpu.VMEM((ROWS, WIN), F32),
        pltpu.VMEM((CHIPS, ROWS, WIN), BF16),
        pltpu.VMEM((CHIPS, ROWS, WIN), F32),
        pltpu.VMEM((CHIPS,) + tile, F32),
        pltpu.VMEM((CHIPS,) + tile, F32),
        pltpu.VMEM(tile, F32),
        pltpu.VMEM((CHIPS,) + tile, BF16),
        pltpu.VMEM((HEADS,) + tile, BF16),
        pltpu.VMEM((HEADS, 4, CHIPS, ROWS), F32),
        pltpu.VMEM((4, CHIPS, ROWS), F32),
        pltpu.VMEM((CHIPS,) + tile, BF16),
        pltpu.VMEM((ROWS, WIDTH), BF16),
        pltpu.VMEM((8,) + tile, BF16),
        pltpu.VMEM((8,) + tile, BF16),
        pltpu.VMEM((16, 16, WIDTH // 2), BF16),
        pltpu.VMEM((16, 16, WIDTH // 2), BF16),
        pltpu.VMEM((2 * ROWS, 2 * ROWS), BF16),
        pltpu.VMEM((ROWS, 2 * ROWS), F32),
        pltpu.VMEM((padded, 2 * ROWS), F32),
        pltpu.VMEM((ROWS, WIN), F32),
        pltpu.VMEM(tile, F32),
        pltpu.VMEM(tile, F32),
        pltpu.VMEM((CHIPS,) + tile, BF16),
        pltpu.VMEM((CHIPS, ROWS, 2 * ROWS), BF16),
        pltpu.VMEM((CHIPS, ROWS, 2 * ROWS), BF16),
        pltpu.VMEM((CHIPS, 2) + tile, BF16),
        pltpu.VMEM((8, 8, ROWS), F32),
        pltpu.VMEM((16, 8, ROWS), F32),
        dma((8,)),
    ] + [
        dma((count,))
        for count in (
            8, 8, 8, 8, 8, 8, 8, 8, 8, 8, 1, 1, 8, 8, 8, 8,
            4, 4, 4, 4, 8, 8, 16, 16, 8, 8, 8, 8, 8, 8, 16, 16,
        )
    ]
    partial = pl.pallas_call(
        kernel,
        out_shape=(
            jax.ShapeDtypeStruct((ROWS, WIDTH), BF16),
            jax.ShapeDtypeStruct((ROWS, WIDTH), BF16),
            jax.ShapeDtypeStruct((HEADS,) + tile, BF16),
            jax.ShapeDtypeStruct((HEADS, 2) + tile, BF16),
            jax.ShapeDtypeStruct((8, WIDTH), F32),
            jax.ShapeDtypeStruct((1, WIDTH), F32),
            jax.ShapeDtypeStruct((HEADS, BUCKETS), F32),
            jax.ShapeDtypeStruct((HEADS, BUCKETS), F32),
        ),
        in_specs=[hbm, hbm, sm, vm, sm, sm, vm, hbm, hbm],
        out_specs=(hbm,) * 4 + (vm,) * 4,
        scratch_shapes=scratch,
        compiler_params=pltpu.CompilerParams(
            collective_id=0, has_side_effects=True, vmem_limit_bytes=63 * 1024 * 1024
        ),
    )(
        uvqk[0], residual[0], lengths, time_buckets, pos_table, time_table,
        output_norm_gain[None], w_out, cotangent[0],
    )
    steps = 2
    some = ROWS // steps

    def whole(*shape):
        return pl.BlockSpec(shape, lambda i: (0,) * len(shape))

    wide = pl.BlockSpec((some, 4 * WIDTH), lambda i: (i, 0))
    narrow = pl.BlockSpec((some, WIDTH), lambda i: (i, 0))
    small = [whole(8, WIDTH), whole(1, WIDTH), whole(HEADS, BUCKETS), whole(HEADS, BUCKETS)]
    out, dpre, dwo, dgain, dpos, dtime = pl.pallas_call(
        finish,
        grid=(steps,),
        out_shape=(
            jax.ShapeDtypeStruct((ROWS, WIDTH), BF16),
            jax.ShapeDtypeStruct((ROWS, 4 * WIDTH), BF16),
            jax.ShapeDtypeStruct((8, WIDTH), F32),
            jax.ShapeDtypeStruct((1, WIDTH), F32),
            jax.ShapeDtypeStruct((HEADS, BUCKETS), F32),
            jax.ShapeDtypeStruct((HEADS, BUCKETS), F32),
        ),
        in_specs=[
            wide, narrow, narrow,
            pl.BlockSpec((HEADS, some, ROWS), lambda i: (0, i, 0)),
            pl.BlockSpec((HEADS, 2, some, ROWS), lambda i: (0, 0, i, 0)),
        ] + small,
        out_specs=[narrow, wide] + small,
        compiler_params=pltpu.CompilerParams(vmem_limit_bytes=63 * 1024 * 1024),
    )(uvqk[0], *partial)
    return (out[None], dpre[None], dwo, dgain[0], dpos, dtime)


def solution(mesh):
    in_specs = (
        P("dp", "ctx", None),
        P("dp", "ctx", None),
        P("dp", None),
        P("dp", "ctx"),
        P(),
        P(),
        P(),
        P(),
        P("dp", "ctx", None),
    )
    out_specs = (P("dp", "ctx", None), P("dp", "ctx", None), P(("dp", "ctx"), None), P(), P(), P())
    return jax.shard_map(body, mesh=mesh, in_specs=in_specs, out_specs=out_specs, check_vma=False)
```
